32 devices in a mesh: grp: 2 (over y), dp: 16 (over z, x, core).
Axes of the slice: x: 2, y: 2, z: 4, core: 2. Of those that a mesh axis runs over, the one named last changes fastest.
Arguments:
- acts: bfloat16 [16384, 2560], P(('grp', 'dp')), may hold values from -18 to 18
- cotangents: bfloat16 [16384, 768], P(('grp', 'dp')), may hold values from -6 to 6
Outputs:
- update: float32 [2560, 768], P(('grp', 'dp'))
The draws below stay inside these ranges and needn't reach their ends.
All inputs are finite; a program needn't handle non-finite values. Where the reference program divides by a largest or mean magnitude, that divisor is 1e-20 or more.
Results may differ from the reference program's by a relative error of at most 0.013.
Values may be sent and summed in bfloat16 or wider, within the bound.
A program may use at most 64 MiB of HBM per device.

```python
import jax
import jax.numpy as jnp
from jax import lax

D = 2560
R = 768
BLK = 128
ITERS = 8
TOK_DEV = 512
TOKENS = 16384
NA = 20
NG = 6


def draw_acts(key, part):
    key_vals = jax.random.fold_in(key, 11)
    key_perm = jax.random.fold_in(key, 23)
    devcount = TOKENS // TOK_DEV
    span = D // devcount
    values = jnp.clip(jax.random.normal(key_vals, (TOKENS, D), jnp.float32), -6.0, 6.0)
    slope = 0.5
    column = jnp.arange(D, dtype=jnp.float32)
    col_scale = jnp.power(10.0, -slope * column / D)
    paired = jax.random.permutation(key_perm, devcount)
    row_dev = jnp.arange(TOKENS, dtype=jnp.int32) // TOK_DEV
    col_block = jnp.arange(D, dtype=jnp.int32) // span
    spike = jnp.where(paired[row_dev][:, None] == col_block[None, :], 3.0, 1.0)
    return (values * spike * col_scale[None, :]).astype(jnp.bfloat16)


def level_of(key, shape, split, low, largest):
    level, own = 1.0, jax.random.fold_in(key, 6)
    for dim, parts in split:
        draws = jnp.exp(jax.random.uniform(jax.random.fold_in(own, dim), (parts,), jnp.float32, low / len(split), largest / len(split)))
        level = level * jnp.repeat(draws, shape[dim] // parts).reshape([-1 if axis == dim else 1 for axis in range(len(shape))])
    return level


def normal_values(stream_key, dims, scale, reach, cuts=(), kind=jnp.bfloat16):
    result = jax.random.normal(stream_key, dims, jnp.float32) * scale
    if len(cuts) > 0:
        result = level_of(stream_key, dims, cuts, -0.22, 0.18) * result
    return jnp.clip(result, min=-reach, max=reach).astype(kind)


def setup_inputs(seed: int = 0) -> dict:
    streams_of = jax.random.split(jax.random.key(seed), 3)
    return {
        "acts": draw_acts(jax.random.fold_in(streams_of[2], 71), 0),
        "cotangents": normal_values(streams_of[1], (TOKENS, R), 1.0, 6.0, ((0, 32),)),
    }


def newton_inverse(blocks):
    eye = jnp.eye(BLK, dtype=jnp.float32)
    trace = lax.optimization_barrier(jnp.sum(blocks * eye, axis=(1, 2)))
    damped = blocks + (0.1 * (trace / BLK + 1e-06))[:, None, None] * eye
    scale = 1.0 / lax.optimization_barrier(jnp.max(lax.optimization_barrier(jnp.sum(jnp.abs(damped), axis=2)), axis=1))
    approx = scale[:, None, None] * eye
    for step in range(ITERS):
        product = jnp.einsum('nij,njk->nik', damped, approx, precision=lax.Precision.HIGHEST)
        approx = jnp.einsum('nij,njk->nik', approx, 2.0 * eye - product, precision=lax.Precision.HIGHEST)
    return approx

def reference(acts, cotangents):
    tokens = acts.shape[0]
    x_blocks = acts.astype(jnp.float32).reshape(tokens, NA, BLK)
    d_blocks = cotangents.astype(jnp.float32).reshape(tokens, NG, BLK)
    fa = jnp.einsum('tbi,tbj->bij', x_blocks, x_blocks, precision=lax.Precision.HIGHEST) / TOKENS
    fg = jnp.einsum('tbi,tbj->bij', d_blocks, d_blocks, precision=lax.Precision.HIGHEST) / TOKENS
    inverse16 = newton_inverse(jnp.concatenate([fa, fg], axis=0)).astype(jnp.bfloat16).astype(jnp.float32)
    xpre = jnp.einsum('tbi,bij->tbj', x_blocks, inverse16[:NA], precision=lax.Precision.HIGHEST)
    xpre = xpre.astype(jnp.bfloat16).reshape(tokens, D)
    left = jnp.dot(xpre.T, cotangents, preferred_element_type=jnp.float32) / TOKENS
    natural = jnp.einsum('rci,cij->rcj', left.reshape(D, NG, BLK), inverse16[NA:], precision=lax.Precision.HIGHEST).reshape(D, R)
    quad = jnp.mean(natural * natural)
    return natural / jnp.sqrt(quad + 1e-06)
```

```python
import functools

import jax
import jax.numpy as jnp
from jax import lax
from jax.experimental import pallas as pl
from jax.experimental.pallas import tpu as pltpu
from jax.sharding import PartitionSpec as P

D = 2560
R = 768
BLK = 128
ITERS = 8
NA = D // BLK
NG = R // BLK
QROWS = D // 4
QBLK = QROWS // BLK
CH = 4
PART = BLK // CH
SUB = PART // 2
SROWS = QBLK * SUB
CCOLS = R // 2
CBLK = CCOLS // BLK
SLOTS = 4
MESH = pl.DeviceIdType.MESH
F32 = jnp.float32
BF16 = jnp.bfloat16


def dot(a, b):
    return jnp.dot(a, b, preferred_element_type=F32)


def dot_t(a, b):
    return lax.dot_general(a, b, (((0,), (0,)), ((), ())), preferred_element_type=F32)


def split(a):
    hi = a.astype(BF16)
    return hi, (a - hi.astype(F32)).astype(BF16)


def dot3(a, b):
    ah, al = split(a)
    bh, bl = split(b)
    both = dot(
        jnp.concatenate([ah, al], axis=1),
        jnp.concatenate(
            [jnp.concatenate([bh, bl], axis=1), jnp.concatenate([bh, jnp.zeros_like(bh)], axis=1)],
            axis=0,
        ),
    )
    return both[:, :BLK] + both[:, BLK:]


def kernel(
    groups, width, total, rows,
    x_hbm, g_hbm, out_ref,
    x_ref, g_ref, xt, fpart, f1recv, f2send, f2recv, f3send, f3recv,
    m1send, m1recv, mown, masend, m2a, mbsend, m2b,
    zsend, zrecv, inv_own, inv_a, inv_g, nat, fin_send, fin_recv, qsend, q1recv, q2recv,
    in_sem,
    f1_ss, f1_rs, f2_ss, f2_rs, f3_ss, f3_rs, m1_ss, m1_rs, ma_ss, ma_rs,
    mb_ss, mb_rs, z_ss, z_rs, inv_ss, inv_rs, fin_ss, fin_rs, q1_ss, q1_rs, q2_ss, q2_rs,
):
    devices = groups * width
    rest_n = devices // 8
    owners = devices // 4
    half_n = devices // 2
    zslots = zsend.shape[1]
    pieces = fin_send.shape[0] // zslots
    dp_rest = width // 4
    gi = lax.axis_index("grp")
    di = lax.axis_index("dp")
    me = gi * width + di
    core = lax.rem(di, 2)
    x = lax.rem(lax.div(di, 2), 2)
    y = lax.rem(gi, 2)
    q = 2 * y + x
    rest = lax.div(gi, 2) * dp_rest + lax.div(di, 4)

    def at(yy, xx, zz, cc):
        return (
            lax.div(zz, dp_rest) * 2 + yy,
            lax.rem(zz, dp_rest) * 4 + xx * 2 + cc,
        )

    def linear(d):
        return (lax.div(d, width), lax.rem(d, width))

    def rcopy(src, dst, ss, rs, dev):
        return pltpu.make_async_remote_copy(
            src_ref=src, dst_ref=dst, send_sem=ss, recv_sem=rs,
            device_id=dev, device_id_type=MESH,
        )

    g_in = pltpu.make_async_copy(g_hbm, g_ref, in_sem.at[4])
    g_in.start()
    x_in = []
    for i in range(4):
        cols = pl.ds(i * QROWS, QROWS)
        x_in.append(pltpu.make_async_copy(x_hbm.at[:, cols], x_ref.at[:, cols], in_sem.at[i]))
        x_in[i].start()

    barrier = pltpu.get_barrier_semaphore()

    def greet(dev):
        pl.semaphore_signal(barrier, inc=1, device_id=dev, device_id_type=MESH)

    greet(at(y, x, rest, 1 - core))
    for yy, xx in ((y, 1 - x), (1 - y, x), (1 - y, 1 - x)):
        greet(at(yy, xx, rest, core))

    @pl.loop(0, rest_n)
    def _(z):
        @pl.when(z != rest)
        def _():
            greet(at(y, x, z, core))

    zero = jnp.zeros((BLK, BLK), BF16)
    g_in.wait()
    g_other = g_ref[:, pl.ds(pl.multiple_of((1 - core) * CCOLS, BLK), CCOLS)]
    g_mine = g_ref[:, pl.ds(pl.multiple_of(core * CCOLS, BLK), CCOLS)]
    for i in range(QBLK * CBLK, zslots * rest_n):
        for k in range(CH):
            zsend[k, i // zslots, i % zslots] = zero[:PART]

    def scatter(ref, yq, xq, t, value):
        for k in range(CH):
            for h in range(2):
                major, minor = (xq, yq) if h == 0 else (yq, xq)
                start = k * PART + h * SUB
                ref[k, h, major, minor, t * SUB:(t + 1) * SUB, :] = value[start:start + SUB]

    for part in range(4):
        x_in[part].wait()
        for b in range(part * QBLK, (part + 1) * QBLK):
            yq, xq, t = b // (2 * QBLK), b % 2, b % (2 * QBLK) // 2
            xbt = x_ref[:, b * BLK:(b + 1) * BLK].T
            xt[b] = xbt
            scatter(m1send, yq, xq, t, dot(xbt, g_other).astype(BF16))

    pl.semaphore_wait(barrier, rest_n + 3)
    other = at(y, x, rest, 1 - core)
    at_x = at(y, 1 - x, rest, core)
    at_y = at(1 - y, x, rest, core)
    m1 = [rcopy(m1send.at[k], m1recv.at[k], m1_ss.at[k], m1_rs.at[k], other) for k in range(CH)]
    for cp in m1:
        cp.start()

    for b in range(NA):
        yq, xq, t = b // (2 * QBLK), b % 2, b % (2 * QBLK) // 2
        scatter(mown, yq, xq, t, dot(xt[b], g_mine))

    def summed(k, h, major, minor):
        return mown[k, h, major, minor] + m1recv[k, h, major, minor].astype(F32)

    side = (x, y)
    near = (at_x, at_y)
    ma, mb = {}, {}

    def stage_a(k):
        m1[k].wait_recv()
        for h in range(2):
            for minor in range(2):
                masend[k, h, minor] = summed(k, h, 1 - side[h], minor).astype(BF16)
            ma[k, h] = rcopy(
                masend.at[k, h], m2a.at[k, h], ma_ss.at[2 * k + h], ma_rs.at[2 * k + h], near[h]
            )
            ma[k, h].start()

    def stage_b(k):
        for h in range(2):
            ma[k, h].wait_recv()
            minor = 1 - side[1 - h]
            mbsend[k, h] = (
                summed(k, h, side[h], minor) + m2a[k, h, minor].astype(F32)
            ).astype(BF16)
            mb[k, h] = rcopy(
                mbsend.at[k, h], m2b.at[k, h], mb_ss.at[2 * k + h], mb_rs.at[2 * k + h], near[1 - h]
            )
            mb[k, h].start()

    def z_copy(k, dst, src):
        return rcopy(
            zsend.at[k, dst], zrecv.at[k, src],
            z_ss.at[k * rest_n + dst], z_rs.at[k * rest_n + src], at(y, x, dst, core),
        )

    def stage_z(k):
        for h in range(2):
            mb[k, h].wait_recv()
            minor = side[1 - h]
            value = (
                summed(k, h, side[h], minor) + m2a[k, h, minor].astype(F32) + m2b[k, h].astype(F32)
            ) * (1.0 / total)
            value = value.astype(BF16)
            for i in range(QBLK * CBLK):
                t, c = divmod(i, CBLK)
                zsend[k, i // zslots, i % zslots, h * SUB:(h + 1) * SUB, :] = (
                    value[t * SUB:(t + 1) * SUB, c * BLK:(c + 1) * BLK]
                )

        @pl.loop(0, rest_n)
        def _(z):
            @pl.when(z != rest)
            def _():
                z_copy(k, z, rest).start()

        zrecv[k, rest] = zsend[k, rest]

    stage_a(0)

    for c in range(NG):
        gb = g_ref[:, c * BLK:(c + 1) * BLK]
        fg = dot_t(gb, gb).astype(BF16)
        if c < 4:
            fpart[1, c, 2] = fg
        else:
            fpart[0, c - 4, 3] = fg
    for c in range(4):
        fpart[1, c, 3] = zero
        if c >= NG - 4:
            fpart[0, c, 3] = zero
    for b in range(NA):
        qq, t = b // (2 * QBLK) * 2 + b % 2, b % (2 * QBLK) // 2
        fpart[t % 2, qq, t // 2] = dot(xt[b], x_ref[:, b * BLK:(b + 1) * BLK]).astype(BF16)
    f1 = rcopy(fpart.at[1 - core], f1recv, f1_ss.at[0], f1_rs.at[0], other)
    f1.start()

    stage_a(1)
    f1.wait_recv()

    def f1_sum(qq, s):
        return fpart[core, qq, s].astype(F32) + f1recv[qq, s].astype(F32)

    chips = [(y, 1 - x), (1 - y, x), (1 - y, 1 - x)]
    f2 = []
    for k, (yy, xx) in enumerate(chips):
        qq = 2 * yy + xx
        for s in range(SLOTS):
            f2send[k, s] = f1_sum(qq, s).astype(BF16)
        c2 = rcopy(f2send.at[k], f2recv.at[k], f2_ss.at[k], f2_rs.at[k], at(yy, xx, rest, core))
        c2.start()
        f2.append(c2)

    stage_a(2)
    stage_a(3)
    stage_b(0)

    for c2 in f2:
        c2.wait_recv()
    for s in range(SLOTS):
        f = f1_sum(q, s)
        for k in range(3):
            f = f + f2recv[k, s].astype(F32)
        f3send[s] = f.astype(BF16)

    def f3_copy(s, src):
        return rcopy(f3send.at[s], f3recv.at[src], f3_ss.at[s], f3_rs.at[src], at(y, x, s, core))

    for s in range(SLOTS):
        @pl.when(rest != s)
        def _():
            f3_copy(s, rest).start()

    f3recv[rest] = f3send[lax.rem(rest, SLOTS)]

    stage_b(1)
    stage_z(0)

    @pl.when(rest < SLOTS)
    def _():
        @pl.loop(0, rest_n)
        def _(z):
            @pl.when(z != rest)
            def _():
                f3_copy(0, z).wait_recv()

    if rest_n > SLOTS:
        @pl.when(rest >= SLOTS)
        def _():
            @pl.loop(0, rest_n)
            def _(z):
                f3recv[z] = zero

    factor = f3recv[0].astype(F32)
    for z in range(1, rest_n):
        factor = factor + f3recv[z].astype(F32)
    factor = factor * (1.0 / total)

    eye = (
        lax.broadcasted_iota(jnp.int32, (BLK, BLK), 0)
        == lax.broadcasted_iota(jnp.int32, (BLK, BLK), 1)
    ).astype(F32)
    trace = jnp.sum(jnp.sum(factor * eye, axis=1, keepdims=True), axis=0, keepdims=True)
    damped = factor + (0.1 * (trace / BLK + 1e-06)) * eye
    peak = jnp.max(jnp.sum(jnp.abs(damped), axis=1, keepdims=True), axis=0, keepdims=True)
    scale = 1.0 / peak
    power = eye - scale * damped
    approx = scale * (eye + power)
    power = dot3(power, power)

    def steps(n, power, approx):
        for _ in range(n):
            both = dot3(jnp.concatenate([power, approx], axis=0), power)
            power, approx = both[:BLK], approx + both[BLK:]
        return power, approx

    power, approx = steps(2, power, approx)
    stage_b(2)
    stage_z(1)
    power, approx = steps(4, power, approx)
    approx = approx + dot3(approx, power)
    inv_own[...] = approx.astype(BF16)
    stage_b(3)
    stage_z(2)

    slot = 2 * rest + core
    is_a = slot < QBLK
    is_g = jnp.logical_or(slot == QBLK, jnp.logical_and(slot == QBLK + 1, q < NG - 4))
    gidx = (slot - QBLK) * 4 + q
    ghalf = lax.div(gidx, CBLK)

    def a_copy(i, t):
        return rcopy(
            inv_own, inv_a.at[t], inv_ss.at[i], inv_rs.at[t],
            at(y, x, lax.div(i, 2), lax.rem(i, 2)),
        )

    def g_dev(i):
        chip = lax.div(i, rest_n)
        return at(lax.div(chip, 2), lax.rem(chip, 2), lax.rem(i, rest_n), ghalf)

    def g_copy(i, c):
        return rcopy(inv_own, inv_g.at[c], inv_ss.at[i], inv_rs.at[QBLK + c], g_dev(i))

    def not_me(i):
        gg, dd = g_dev(i)
        return gg * width + dd != me

    @pl.when(is_a)
    def _():
        @pl.loop(0, owners)
        def _(i):
            @pl.when(i != slot)
            def _():
                a_copy(i, slot).start()
        inv_a[slot] = inv_own[...]

    @pl.when(is_g)
    def _():
        @pl.loop(0, 4 * rest_n)
        def _(i):
            @pl.when(not_me(i))
            def _():
                g_copy(i, lax.rem(gidx, CBLK)).start()

        @pl.when(ghalf == core)
        def _():
            inv_g[lax.rem(gidx, CBLK)] = inv_own[...]

    stage_z(3)

    for c in range(CBLK):
        @pl.when(jnp.logical_not(jnp.logical_and(is_g, gidx == core * CBLK + c)))
        def _():
            g_copy(0, c).wait_recv()
    for t in range(QBLK):
        @pl.when(slot != t)
        def _():
            a_copy(0, t).wait_recv()

    @pl.loop(0, rest_n)
    def _(z):
        @pl.when(z != rest)
        def _():
            for k in range(CH):
                z_copy(k, 0, z).wait_recv()

    square = jnp.zeros((1, 1), F32)
    for k in range(zslots):
        tile = rest * zslots + k
        m = jnp.concatenate(
            [sum(zrecv[j, z, k].astype(F32) for z in range(rest_n)) for j in range(CH)], axis=0
        )
        left = dot_t(inv_a[jnp.minimum(lax.div(tile, CBLK), QBLK - 1)], m.astype(BF16))
        hi, lo = split(left)
        ginv = inv_g[lax.rem(tile, CBLK)]
        part = dot(hi, ginv) + dot(lo, ginv)
        nat[k] = part
        square = square + jnp.sum(
            jnp.sum(part * part, axis=0, keepdims=True), axis=1, keepdims=True
        )
    qsend[0] = jnp.broadcast_to(square, (8, 128))

    def q1_copy(p, src):
        return rcopy(
            qsend.at[0], q1recv.at[src], q1_ss.at[p], q1_rs.at[src],
            at(lax.div(p, 4), lax.rem(lax.div(p, 2), 2), rest, lax.rem(p, 2)),
        )

    def q2_copy(z, src):
        return rcopy(qsend.at[1], q2recv.at[src], q2_ss.at[z], q2_rs.at[src], at(y, x, z, core))

    plane = 2 * q + core

    def others(n, mine, body):
        @pl.loop(0, n)
        def _(p):
            @pl.when(p != mine)
            def _():
                body(p)

    others(8, plane, lambda p: q1_copy(p, plane).start())
    q1recv[plane] = qsend[0]

    def each_piece(body):
        for xx in range(2):
            for i in range(QBLK * CBLK):
                t, c = divmod(i, CBLK)
                top = (2 * t + xx) * BLK

                @pl.when(jnp.logical_and(x == xx, rest == i // zslots))
                def _():
                    first = top // rows
                    for k in range(first, (top + BLK + rows - 1) // rows):
                        lo, hi = max(top, k * rows), min(top + BLK, (k + 1) * rows)
                        late = 0 if lo == k * rows else 1
                        body(i % zslots, c, k, lo - k * rows, lo - top, hi - lo, late,
                             i % zslots * pieces + k - first)

    def fin_copy(j, c, late, k):
        return rcopy(
            fin_send.at[j], fin_recv.at[core * CBLK + c, late], fin_ss.at[j],
            fin_rs.at[2 * (core * CBLK + c) + late], linear(y * half_n + k),
        )

    def send_piece(slot_k, c, k, above, start, count, late, j):
        parts = [nat[slot_k, start:start + count, :]]
        if above:
            parts.insert(0, jnp.zeros((above, BLK), F32))
        tail = fin_send.shape[1] - above - count
        if tail:
            parts.append(jnp.zeros((tail, BLK), F32))
        fin_send[j] = (jnp.concatenate(parts, axis=0) if len(parts) > 1 else parts[0]).astype(BF16)

        @pl.when(y * half_n + k != me)
        def _():
            fin_copy(j, c, late, k).start()

        @pl.when(y * half_n + k == me)
        def _():
            fin_recv[core * CBLK + c, late] = fin_send[j]

    each_piece(send_piece)

    others(8, plane, lambda p: q1_copy(0, p).wait_recv())
    qsend[1] = jnp.sum(q1recv[...], axis=0)
    others(rest_n, rest, lambda z: q2_copy(z, rest).start())
    q2recv[rest] = qsend[1]

    k_me = lax.rem(me, half_n)
    t_me = lax.div(k_me * rows, BLK)
    straddles = lax.div(k_me * rows + rows - 1, BLK) > t_me
    mine_here = lax.div(me, half_n) == y
    for late in range(2):
        for c in range(NG):
            from_me = jnp.logical_and(
                jnp.logical_and(mine_here, core == c // CBLK),
                jnp.logical_and(
                    lax.rem(t_me + late, 2) == x,
                    lax.div(CBLK * lax.div(t_me + late, 2) + c % CBLK, zslots) == rest,
                ),
            )
            incoming = jnp.logical_not(from_me)
            if late:
                incoming = jnp.logical_and(straddles, incoming)

                @pl.when(jnp.logical_not(straddles))
                def _():
                    fin_recv[c, 1] = jnp.zeros(fin_recv.shape[2:], BF16)

            @pl.when(incoming)
            def _():
                pltpu.make_async_remote_copy(
                    src_ref=fin_send.at[0], dst_ref=fin_recv.at[c, late], send_sem=fin_ss.at[0],
                    recv_sem=fin_rs.at[2 * c + late], device_id=other, device_id_type=MESH,
                ).wait_recv()

    others(rest_n, rest, lambda z: q2_copy(0, z).wait_recv())
    quad = jnp.sum(q2recv[...], axis=0)[:1, :1] / (D * R)
    factor_out = lax.rsqrt(quad + 1e-06)
    for c in range(NG):
        natural = fin_recv[c, 0].astype(F32) + fin_recv[c, 1].astype(F32)
        out_ref[:, c * BLK:(c + 1) * BLK] = natural[:rows, :] * factor_out

    f1.wait_send()
    for cp in f2 + m1 + list(ma.values()) + list(mb.values()):
        cp.wait_send()

    for s in range(SLOTS):
        @pl.when(rest != s)
        def _():
            f3_copy(s, rest).wait_send()

    @pl.when(is_a)
    def _():
        @pl.loop(0, owners)
        def _(i):
            @pl.when(i != slot)
            def _():
                a_copy(i, 0).wait_send()

    @pl.when(is_g)
    def _():
        @pl.loop(0, 4 * rest_n)
        def _(i):
            @pl.when(not_me(i))
            def _():
                g_copy(i, 0).wait_send()

    for k in range(CH):
        others(rest_n, rest, lambda z: z_copy(k, z, 0).wait_send())
    others(8, plane, lambda p: q1_copy(p, 0).wait_send())
    others(rest_n, rest, lambda z: q2_copy(z, 0).wait_send())

    def wait_piece(slot_k, c, k, above, start, count, late, j):
        @pl.when(y * half_n + k != me)
        def _():
            fin_copy(j, c, late, k).wait_send()

    each_piece(wait_piece)


def per_device(acts, cotangents, groups, width):
    tokens = acts.shape[0]
    devices = groups * width
    rest_n = devices // 8
    owners = devices // 4
    rows = D // devices
    padded = (rows + 15) // 16 * 16
    blk = (BLK, BLK)
    zslots = (QBLK * CBLK + rest_n - 1) // rest_n
    pieces = max(
        ((t + 1) * BLK + rows - 1) // rows - t * BLK // rows for t in range(2 * QBLK)
    )
    sems = [5, 1, 1, 3, 3, SLOTS, rest_n, CH, CH, 2 * CH, 2 * CH, 2 * CH, 2 * CH,
            CH * rest_n, CH * rest_n, max(owners, 4 * rest_n),
            QBLK + CBLK, zslots * pieces, 2 * NG, 8, 8, rest_n, rest_n]
    vm = pltpu.VMEM
    return pl.pallas_call(
        functools.partial(kernel, groups, width, tokens * devices, rows),
        out_shape=jax.ShapeDtypeStruct((rows, R), F32),
        in_specs=[pl.BlockSpec(memory_space=pl.ANY)] * 2,
        out_specs=pl.BlockSpec(memory_space=pltpu.VMEM),
        scratch_shapes=[
            vm((tokens, D), BF16),
            vm((tokens, R), BF16),
            vm((NA, BLK, tokens), BF16),
            vm((2, 4, SLOTS) + blk, BF16),
            vm((4, SLOTS) + blk, BF16),
            vm((3, SLOTS) + blk, BF16),
            vm((3, SLOTS) + blk, BF16),
            vm((SLOTS,) + blk, BF16),
            vm((rest_n,) + blk, BF16),
            vm((CH, 2, 2, 2, SROWS, CCOLS), BF16),
            vm((CH, 2, 2, 2, SROWS, CCOLS), BF16),
            vm((CH, 2, 2, 2, SROWS, CCOLS), F32),
            vm((CH, 2, 2, SROWS, CCOLS), BF16),
            vm((CH, 2, 2, SROWS, CCOLS), BF16),
            vm((CH, 2, SROWS, CCOLS), BF16),
            vm((CH, 2, SROWS, CCOLS), BF16),
            vm((CH, rest_n, zslots, PART, BLK), BF16),
            vm((CH, rest_n, zslots, PART, BLK), BF16),
            vm(blk, BF16),
            vm((QBLK,) + blk, BF16),
            vm((CBLK,) + blk, BF16),
            vm((zslots,) + blk, F32),
            vm((zslots * pieces, padded, BLK), BF16),
            vm((NG, 2, padded, BLK), BF16),
            vm((2, 8, 128), F32),
            vm((8, 8, 128), F32),
            vm((rest_n, 8, 128), F32),
        ] + [pltpu.SemaphoreType.DMA((n,)) for n in sems],
        compiler_params=pltpu.CompilerParams(
            collective_id=0, has_side_effects=True, vmem_limit_bytes=63 * 1024 * 1024
        ),
    )(acts, cotangents)


def solution(mesh):
    groups, width = mesh.shape["grp"], mesh.shape["dp"]
    spec = P(("grp", "dp"), None)
    return jax.shard_map(
        functools.partial(per_device, groups=groups, width=width),
        mesh=mesh, in_specs=(spec, spec), out_specs=spec, check_vma=False,
    )
```

```python
import functools

import jax
import jax.numpy as jnp
from jax import lax
from jax.experimental import pallas as pl
from jax.experimental.pallas import tpu as pltpu
from jax.sharding import PartitionSpec as P

D = 2560
R = 768
BLK = 128
ITERS = 8
NA = D // BLK
NG = R // BLK
QROWS = D // 4
QBLK = QROWS // BLK
CH = 4
PART = BLK // CH
SUB = PART // 2
SROWS = QBLK * SUB
CCOLS = R // 2
CBLK = CCOLS // BLK
PROWS = BLK + 16
A_OWNER = ((0, 1, 0), (0, 1, 1), (1, 2, 0), (1, 2, 1), (0, 2, 0))
G_OWNER = ((0, 2, 1), (1, 1, 0))
MESH = pl.DeviceIdType.MESH
F32 = jnp.float32
BF16 = jnp.bfloat16


def dot(a, b):
    return jnp.dot(a, b, preferred_element_type=F32)


def dot_t(a, b):
    return lax.dot_general(a, b, (((0,), (0,)), ((), ())), preferred_element_type=F32)


def split(a):
    hi = a.astype(BF16)
    return hi, (a - hi.astype(F32)).astype(BF16)


def dot3(a, b):
    ah, al = split(a)
    bh, bl = split(b)
    both = dot(
        jnp.concatenate([ah, al], axis=1),
        jnp.concatenate(
            [jnp.concatenate([bh, bl], axis=1), jnp.concatenate([bh, jnp.zeros_like(bh)], axis=1)],
            axis=0,
        ),
    )
    return both[:, :BLK] + both[:, BLK:]


def kernel(
    groups, width, total, rows,
    x_hbm, g_hbm, out_ref,
    x_ref, g_ref, xt, fpart, f1recv, f2send, f2recv, f3send, f3recv,
    m1send, m1recv, mown, masend, m2a, mbsend, m2b,
    zsend, zrecv, state, inv_own, inv_a, inv_g, nat, fin_send, fin_recv, qsend, q1recv, q2recv,
    in_sem,
    f1_ss, f1_rs, f2_ss, f2_rs, f3_ss, f3_rs, m1_ss, m1_rs, ma_ss, ma_rs,
    mb_ss, mb_rs, z_ss, z_rs, inv_ss, inv_rs, gz_ss, gp_ss, g_rs, fin_ss, fin_rs, q1_ss, q1_rs, q2_ss, q2_rs,
):
    devices = groups * width
    rest_n = devices // 8
    half_n = devices // 2
    zslots = zsend.shape[1]
    pieces = fin_send.shape[0] // zslots
    dp_rest = width // 4
    gi = lax.axis_index("grp")
    di = lax.axis_index("dp")
    me = gi * width + di
    core = lax.rem(di, 2)
    x = lax.rem(lax.div(di, 2), 2)
    y = lax.rem(gi, 2)
    q = 2 * y + x
    rest = lax.div(gi, 2) * dp_rest + lax.div(di, 4)

    def at(yy, xx, zz, cc):
        return (
            lax.div(zz, dp_rest) * 2 + yy,
            lax.rem(zz, dp_rest) * 4 + xx * 2 + cc,
        )

    def linear(d):
        return (lax.div(d, width), lax.rem(d, width))

    def rcopy(src, dst, ss, rs, dev):
        return pltpu.make_async_remote_copy(
            src_ref=src, dst_ref=dst, send_sem=ss, recv_sem=rs,
            device_id=dev, device_id_type=MESH,
        )

    g_in = pltpu.make_async_copy(g_hbm, g_ref, in_sem.at[4])
    g_in.start()
    x_in = []
    for i in range(4):
        cols = pl.ds(i * QROWS, QROWS)
        x_in.append(pltpu.make_async_copy(x_hbm.at[:, cols], x_ref.at[:, cols], in_sem.at[i]))
        x_in[i].start()

    barrier = pltpu.get_barrier_semaphore()

    def greet(dev):
        pl.semaphore_signal(barrier, inc=1, device_id=dev, device_id_type=MESH)

    greet(at(y, x, rest, 1 - core))
    for yy, xx in ((y, 1 - x), (1 - y, x), (1 - y, 1 - x)):
        greet(at(yy, xx, rest, core))

    @pl.loop(0, rest_n)
    def _(z):
        @pl.when(z != rest)
        def _():
            greet(at(y, x, z, core))

    zero = jnp.zeros((BLK, BLK), BF16)
    g_in.wait()
    g_other = g_ref[:, pl.ds(pl.multiple_of((1 - core) * CCOLS, BLK), CCOLS)]
    g_mine = g_ref[:, pl.ds(pl.multiple_of(core * CCOLS, BLK), CCOLS)]
    for i in range(QBLK * CBLK, zslots * rest_n):
        for k in range(CH):
            zsend[k, i // zslots, i % zslots] = zero[:PART]

    def scatter(ref, yq, xq, t, value):
        for k in range(CH):
            for h in range(2):
                major, minor = (xq, yq) if h == 0 else (yq, xq)
                start = k * PART + h * SUB
                ref[k, h, major, minor, t * SUB:(t + 1) * SUB, :] = value[start:start + SUB]

    if zslots * rest_n > QBLK * CBLK:
        @pl.when(rest * zslots >= QBLK * CBLK)
        def _():
            inv_a[QBLK - 1] = zero

    row = lax.broadcasted_iota(jnp.int32, (BLK, BLK), 0)
    col = lax.broadcasted_iota(jnp.int32, (BLK, BLK), 1)
    eye = (row == col).astype(F32)

    def pack(ref, first, second):
        ref[:BLK, :] = jnp.where(col >= row, first, second).astype(BF16)
        diag = jnp.sum(second * eye, axis=0, keepdims=True)
        ref[BLK:, :] = jnp.broadcast_to(diag, (PROWS - BLK, BLK)).astype(BF16)

    def gram(c):
        gb = g_ref[:, c * BLK:(c + 1) * BLK]
        return dot_t(gb, gb)

    for qq in range(NG - 4):
        last = gram(4 + qq)
        pack(fpart.at[1, qq, 0], last, last)
    for qq in range(NG - 4, 4):
        fpart[1, qq, 0] = jnp.zeros((PROWS, BLK), BF16)

    held = {}
    for part in range(4):
        x_in[part].wait()
        for b in range(part * QBLK, (part + 1) * QBLK):
            yq, xq, t = b // (2 * QBLK), b % 2, b % (2 * QBLK) // 2
            qq = 2 * yq + xq
            xb = x_ref[:, b * BLK:(b + 1) * BLK]
            xbt = xb.T
            xt[b] = xbt
            held[t] = held.get(t, {})
            held[t][qq] = dot(xbt, xb)
            if t == 1:
                pack(fpart.at[0, qq, 0], held[0][qq], held[1][qq])
            elif t == 3:
                pack(fpart.at[1, qq, 1], held[2][qq], held[3][qq])
            elif t == 4:
                pack(fpart.at[0, qq, 1], held[4][qq], gram(qq))
    for b in range(NA):
        yq, xq, t = b // (2 * QBLK), b % 2, b % (2 * QBLK) // 2
        scatter(m1send, yq, xq, t, dot(xt[b], g_other).astype(BF16))

    pl.semaphore_wait(barrier, rest_n + 3)
    other = at(y, x, rest, 1 - core)
    at_x = at(y, 1 - x, rest, core)
    at_y = at(1 - y, x, rest, core)
    f1 = rcopy(fpart.at[1 - core], f1recv, f1_ss.at[0], f1_rs.at[0], other)
    f1.start()
    m1 = [rcopy(m1send.at[k], m1recv.at[k], m1_ss.at[k], m1_rs.at[k], other) for k in range(CH)]
    for cp in m1:
        cp.start()

    for b in range(NA):
        yq, xq, t = b // (2 * QBLK), b % 2, b % (2 * QBLK) // 2
        scatter(mown, yq, xq, t, dot(xt[b], g_mine))

    def summed(k, h, major, minor):
        return mown[k, h, major, minor] + m1recv[k, h, major, minor].astype(F32)

    side = (x, y)
    near = (at_x, at_y)
    ma, mb = {}, {}

    def stage_a(k):
        m1[k].wait_recv()
        for h in range(2):
            for minor in range(2):
                masend[k, h, minor] = summed(k, h, 1 - side[h], minor).astype(BF16)
            ma[k, h] = rcopy(
                masend.at[k, h], m2a.at[k, h], ma_ss.at[2 * k + h], ma_rs.at[2 * k + h], near[h]
            )
            ma[k, h].start()

    def stage_b(k):
        for h in range(2):
            ma[k, h].wait_recv()
            minor = 1 - side[1 - h]
            mbsend[k, h] = (
                summed(k, h, side[h], minor) + m2a[k, h, minor].astype(F32)
            ).astype(BF16)
            mb[k, h] = rcopy(
                mbsend.at[k, h], m2b.at[k, h], mb_ss.at[2 * k + h], mb_rs.at[2 * k + h], near[1 - h]
            )
            mb[k, h].start()

    def z_copy(k, dst, src):
        return rcopy(
            zsend.at[k, dst], zrecv.at[k, src],
            z_ss.at[k * rest_n + dst], z_rs.at[k * rest_n + src], at(y, x, dst, core),
        )

    def stage_z(k):
        for h in range(2):
            mb[k, h].wait_recv()
            minor = side[1 - h]
            value = (
                summed(k, h, side[h], minor) + m2a[k, h, minor].astype(F32) + m2b[k, h].astype(F32)
            ) * (1.0 / total)
            value = value.astype(BF16)
            for i in range(QBLK * CBLK):
                t, c = divmod(i, CBLK)
                zsend[k, i // zslots, i % zslots, h * SUB:(h + 1) * SUB, :] = (
                    value[t * SUB:(t + 1) * SUB, c * BLK:(c + 1) * BLK]
                )

        @pl.loop(0, rest_n)
        def _(z):
            @pl.when(z != rest)
            def _():
                z_copy(k, z, rest).start()

        zrecv[k, rest] = zsend[k, rest]

    f1.wait_recv()

    def f1_sum(qq, s):
        return fpart[core, qq, s].astype(F32) + f1recv[qq, s].astype(F32)

    def present(yy, s):
        return True if s == 1 else jnp.logical_or(core == 0, yy == 0)

    chips = [(y, 1 - x), (1 - y, x), (1 - y, 1 - x)]

    def f2_copy(k, s):
        yy, xx = chips[k]
        i = 2 * k + s
        return rcopy(f2send.at[k, s], f2recv.at[k, s], f2_ss.at[i], f2_rs.at[i], at(yy, xx, rest, core))

    for k, (yy, xx) in enumerate(chips):
        for s in range(2):
            @pl.when(present(yy, s))
            def _():
                f2send[k, s] = f1_sum(2 * yy + xx, s).astype(BF16)
                f2_copy(k, s).start()

    def f3_copy(s, src):
        return rcopy(f3send.at[s], f3recv.at[src], f3_ss.at[s], f3_rs.at[src], at(y, x, s + 1, core))

    def stage_f2():
        for s in range(2):
            @pl.when(present(y, s))
            def _():
                f = f1_sum(q, s)
                for k in range(3):
                    f2_copy(k, s).wait_recv()
                    f = f + f2recv[k, s].astype(F32)
                f3send[s] = f.astype(BF16)

                @pl.when(rest != s + 1)
                def _():
                    f3_copy(s, rest).start()

                @pl.when(rest == s + 1)
                def _():
                    f3recv[s + 1] = f3send[s]

    is_owner = jnp.logical_or(
        rest == 2, jnp.logical_and(rest == 1, jnp.logical_or(core == 0, y == 0))
    )

    def advance(n):
        pairs = [(state[i, 0], state[i, 1]) for i in range(2)]
        for _ in range(n):
            done = []
            for power, approx in pairs:
                both = dot3(jnp.concatenate([power, approx], axis=0), power)
                done.append((both[:BLK], approx + both[BLK:]))
            pairs = done
        return pairs

    def stage_f3():
        @pl.when(is_owner)
        def _():
            @pl.loop(0, rest_n)
            def _(z):
                @pl.when(z != rest)
                def _():
                    f3_copy(0, z).wait_recv()

            packed = f3recv[0].astype(F32)
            for z in range(1, rest_n):
                packed = packed + f3recv[z].astype(F32)
            packed = packed * (1.0 / total)
            half = packed[:BLK]
            flip = half.T
            first = jnp.where(col >= row, half, flip)
            second = jnp.where(col > row, flip, jnp.where(col < row, half, packed[BLK:BLK + 1]))
            for i, factor in enumerate((first, second)):
                trace = jnp.sum(jnp.sum(factor * eye, axis=1, keepdims=True), axis=0, keepdims=True)
                damped = factor + (0.1 * (trace / BLK + 1e-06)) * eye
                peak = jnp.max(jnp.sum(jnp.abs(damped), axis=1, keepdims=True), axis=0, keepdims=True)
                scale = 1.0 / peak
                power = eye - scale * damped
                state[i, 1] = scale * (eye + power)
                state[i, 0] = dot3(power, power)

    def stage_newton(n, last):
        @pl.when(is_owner)
        def _():
            for i, (power, approx) in enumerate(advance(n)):
                if last:
                    inv_own[i] = (approx + dot3(approx, power)).astype(BF16)
                else:
                    state[i, 0] = power
                    state[i, 1] = approx

    def owned(owner):
        return jnp.logical_and(core == owner[0], rest == owner[1])

    def needs(t):
        return range(t * CBLK // zslots, (t * CBLK + CBLK - 1) // zslots + 1)

    a_sends = []
    for t in range(QBLK):
        for z in needs(t):
            for cc in range(2):
                if (cc, z) != A_OWNER[t][:2]:
                    a_sends.append((t, z, cc))

    def a_copy(i):
        t, z, cc = a_sends[i]
        return rcopy(inv_own.at[A_OWNER[t][2]], inv_a.at[t], inv_ss.at[i], inv_rs.at[t], at(y, x, z, cc))

    def g_half(e):
        return lax.div(q + 4 * e, CBLK)

    def gz_copy(e, z):
        return rcopy(
            inv_own.at[G_OWNER[e][2]], inv_g.at[lax.rem(q + 4 * e, CBLK)], gz_ss.at[e * rest_n + z],
            g_rs.at[lax.rem(q + 4 * e, CBLK)], at(y, x, z, g_half(e)),
        )

    def each_gz(body):
        for e in range(2):
            @pl.when(owned(G_OWNER[e]) if e == 0 else jnp.logical_and(owned(G_OWNER[e]), q < NG - 4))
            def _():
                @pl.loop(0, rest_n)
                def _(z):
                    @pl.when(jnp.logical_or(z != rest, g_half(e) != core))
                    def _():
                        body(e, z)

    def stage_inv():
        for i, (t, z, cc) in enumerate(a_sends):
            @pl.when(owned(A_OWNER[t]))
            def _():
                a_copy(i).start()
        each_gz(lambda e, z: gz_copy(e, z).start())
        for t in range(QBLK):
            if A_OWNER[t][1] in needs(t):
                @pl.when(owned(A_OWNER[t]))
                def _():
                    inv_a[t] = inv_own[A_OWNER[t][2]]

    def g_home(j):
        return lax.rem(core * CBLK + j, 4)

    def g_owned(j):
        late = core * CBLK + j >= 4
        return jnp.logical_or(
            jnp.logical_and(late, owned(G_OWNER[1])),
            jnp.logical_and(jnp.logical_not(late), owned(G_OWNER[0])),
        )

    def gp_copy(j, k):
        yy, xx = chips[k]
        return rcopy(inv_g.at[j], inv_g.at[j], gp_ss.at[3 * j + k], g_rs.at[j], at(yy, xx, rest, core))

    def stage_relay():
        for j in range(CBLK):
            @pl.when(q == g_home(j))
            def _():
                @pl.when(g_owned(j))
                def _():
                    inv_g[j] = inv_own[1 - core]

                @pl.when(jnp.logical_not(g_owned(j)))
                def _():
                    gp_copy(j, 0).wait_recv()

                for k in range(3):
                    gp_copy(j, k).start()

    stage_a(0)
    stage_a(1)
    stage_f2()
    stage_b(0)
    stage_a(2)
    stage_f3()
    stage_b(1)
    stage_z(0)
    stage_newton(3, False)
    stage_a(3)
    stage_b(2)
    stage_newton(3, True)
    stage_inv()
    stage_z(1)
    stage_b(3)
    stage_z(2)
    stage_relay()
    stage_z(3)

    for j in range(CBLK):
        @pl.when(q != g_home(j))
        def _():
            gp_copy(j, 0).wait_recv()
    for t in range(QBLK):
        @pl.when(jnp.logical_and(
            jnp.logical_and(rest >= needs(t)[0], rest <= needs(t)[-1]),
            jnp.logical_not(owned(A_OWNER[t])),
        ))
        def _():
            rcopy(inv_own.at[0], inv_a.at[t], inv_ss.at[0], inv_rs.at[t], other).wait_recv()

    @pl.loop(0, rest_n)
    def _(z):
        @pl.when(z != rest)
        def _():
            for k in range(CH):
                z_copy(k, 0, z).wait_recv()

    square = jnp.zeros((1, 1), F32)
    for k in range(zslots):
        tile = rest * zslots + k
        m = jnp.concatenate(
            [sum(zrecv[j, z, k].astype(F32) for z in range(rest_n)) for j in range(CH)], axis=0
        )
        left = dot_t(inv_a[jnp.minimum(lax.div(tile, CBLK), QBLK - 1)], m.astype(BF16))
        hi, lo = split(left)
        ginv = inv_g[lax.rem(tile, CBLK)]
        part = dot(hi, ginv) + dot(lo, ginv)
        nat[k] = part
        square = square + jnp.sum(
            jnp.sum(part * part, axis=0, keepdims=True), axis=1, keepdims=True
        )
    qsend[0] = jnp.broadcast_to(square, (8, 128))

    def q1_copy(p, src):
        return rcopy(
            qsend.at[0], q1recv.at[src], q1_ss.at[p], q1_rs.at[src],
            at(lax.div(p, 4), lax.rem(lax.div(p, 2), 2), rest, lax.rem(p, 2)),
        )

    def q2_copy(z, src):
        return rcopy(qsend.at[1], q2recv.at[src], q2_ss.at[z], q2_rs.at[src], at(y, x, z, core))

    plane = 2 * q + core

    def others(n, mine, body):
        @pl.loop(0, n)
        def _(p):
            @pl.when(p != mine)
            def _():
                body(p)

    others(8, plane, lambda p: q1_copy(p, plane).start())
    q1recv[plane] = qsend[0]

    def each_piece(body):
        for xx in range(2):
            for i in range(QBLK * CBLK):
                t, c = divmod(i, CBLK)
                top = (2 * t + xx) * BLK

                @pl.when(jnp.logical_and(x == xx, rest == i // zslots))
                def _():
                    first = top // rows
                    for k in range(first, (top + BLK + rows - 1) // rows):
                        lo, hi = max(top, k * rows), min(top + BLK, (k + 1) * rows)
                        late = 0 if lo == k * rows else 1
                        body(i % zslots, c, k, lo - k * rows, lo - top, hi - lo, late,
                             i % zslots * pieces + k - first)

    def fin_copy(j, c, late, k):
        return rcopy(
            fin_send.at[j], fin_recv.at[core * CBLK + c, late], fin_ss.at[j],
            fin_rs.at[2 * (core * CBLK + c) + late], linear(y * half_n + k),
        )

    def send_piece(slot_k, c, k, above, start, count, late, j):
        parts = [nat[slot_k, start:start + count, :]]
        if above:
            parts.insert(0, jnp.zeros((above, BLK), F32))
        tail = fin_send.shape[1] - above - count
        if tail:
            parts.append(jnp.zeros((tail, BLK), F32))
        fin_send[j] = (jnp.concatenate(parts, axis=0) if len(parts) > 1 else parts[0]).astype(BF16)

        @pl.when(y * half_n + k != me)
        def _():
            fin_copy(j, c, late, k).start()

        @pl.when(y * half_n + k == me)
        def _():
            fin_recv[core * CBLK + c, late] = fin_send[j]

    each_piece(send_piece)

    others(8, plane, lambda p: q1_copy(0, p).wait_recv())
    qsend[1] = jnp.sum(q1recv[...], axis=0)
    others(rest_n, rest, lambda z: q2_copy(z, rest).start())
    q2recv[rest] = qsend[1]

    k_me = lax.rem(me, half_n)
    t_me = lax.div(k_me * rows, BLK)
    straddles = lax.div(k_me * rows + rows - 1, BLK) > t_me
    mine_here = lax.div(me, half_n) == y
    for late in range(2):
        for c in range(NG):
            from_me = jnp.logical_and(
                jnp.logical_and(mine_here, core == c // CBLK),
                jnp.logical_and(
                    lax.rem(t_me + late, 2) == x,
                    lax.div(CBLK * lax.div(t_me + late, 2) + c % CBLK, zslots) == rest,
                ),
            )
            incoming = jnp.logical_not(from_me)
            if late:
                incoming = jnp.logical_and(straddles, incoming)

                @pl.when(jnp.logical_not(straddles))
                def _():
                    fin_recv[c, 1] = jnp.zeros(fin_recv.shape[2:], BF16)

            @pl.when(incoming)
            def _():
                pltpu.make_async_remote_copy(
                    src_ref=fin_send.at[0], dst_ref=fin_recv.at[c, late], send_sem=fin_ss.at[0],
                    recv_sem=fin_rs.at[2 * c + late], device_id=other, device_id_type=MESH,
                ).wait_recv()

    others(rest_n, rest, lambda z: q2_copy(0, z).wait_recv())
    quad = jnp.sum(q2recv[...], axis=0)[:1, :1] / (D * R)
    factor_out = lax.rsqrt(quad + 1e-06)
    for c in range(NG):
        natural = fin_recv[c, 0].astype(F32) + fin_recv[c, 1].astype(F32)
        out_ref[:, c * BLK:(c + 1) * BLK] = natural[:rows, :] * factor_out

    f1.wait_send()
    for cp in m1 + list(ma.values()) + list(mb.values()):
        cp.wait_send()
    for k, (yy, xx) in enumerate(chips):
        for s in range(2):
            @pl.when(present(yy, s))
            def _():
                f2_copy(k, s).wait_send()
    for s in range(2):
        @pl.when(jnp.logical_and(present(y, s), rest != s + 1))
        def _():
            f3_copy(s, rest).wait_send()
    for i, (t, z, cc) in enumerate(a_sends):
        @pl.when(owned(A_OWNER[t]))
        def _():
            a_copy(i).wait_send()
    each_gz(lambda e, z: gz_copy(e, z).wait_send())
    for j in range(CBLK):
        @pl.when(q == g_home(j))
        def _():
            for k in range(3):
                gp_copy(j, k).wait_send()

    for k in range(CH):
        others(rest_n, rest, lambda z: z_copy(k, z, 0).wait_send())
    others(8, plane, lambda p: q1_copy(p, 0).wait_send())
    others(rest_n, rest, lambda z: q2_copy(z, 0).wait_send())

    def wait_piece(slot_k, c, k, above, start, count, late, j):
        @pl.when(y * half_n + k != me)
        def _():
            fin_copy(j, c, late, k).wait_send()

    each_piece(wait_piece)


def per_device(acts, cotangents, groups, width):
    tokens = acts.shape[0]
    devices = groups * width
    rest_n = devices // 8
    rows = D // devices
    padded = (rows + 15) // 16 * 16
    blk = (BLK, BLK)
    zslots = (QBLK * CBLK + rest_n - 1) // rest_n
    pieces = max(
        ((t + 1) * BLK + rows - 1) // rows - t * BLK // rows for t in range(2 * QBLK)
    )
    sems = [5, 1, 1, 6, 6, 2, rest_n, CH, CH, 2 * CH, 2 * CH, 2 * CH, 2 * CH,
            CH * rest_n, CH * rest_n, 2 * CBLK * QBLK, QBLK,
            2 * rest_n, 3 * CBLK, CBLK, zslots * pieces, 2 * NG, 8, 8, rest_n, rest_n]
    vm = pltpu.VMEM
    return pl.pallas_call(
        functools.partial(kernel, groups, width, tokens * devices, rows),
        out_shape=jax.ShapeDtypeStruct((rows, R), F32),
        in_specs=[pl.BlockSpec(memory_space=pl.ANY)] * 2,
        out_specs=pl.BlockSpec(memory_space=pltpu.VMEM),
        scratch_shapes=[
            vm((tokens, D), BF16),
            vm((tokens, R), BF16),
            vm((NA, BLK, tokens), BF16),
            vm((2, 4, 2, PROWS, BLK), BF16),
            vm((4, 2, PROWS, BLK), BF16),
            vm((3, 2, PROWS, BLK), BF16),
            vm((3, 2, PROWS, BLK), BF16),
            vm((2, PROWS, BLK), BF16),
            vm((rest_n, PROWS, BLK), BF16),
            vm((CH, 2, 2, 2, SROWS, CCOLS), BF16),
            vm((CH, 2, 2, 2, SROWS, CCOLS), BF16),
            vm((CH, 2, 2, 2, SROWS, CCOLS), F32),
            vm((CH, 2, 2, SROWS, CCOLS), BF16),
            vm((CH, 2, 2, SROWS, CCOLS), BF16),
            vm((CH, 2, SROWS, CCOLS), BF16),
            vm((CH, 2, SROWS, CCOLS), BF16),
            vm((CH, rest_n, zslots, PART, BLK), BF16),
            vm((CH, rest_n, zslots, PART, BLK), BF16),
            vm((2, 2) + blk, F32),
            vm((2,) + blk, BF16),
            vm((QBLK,) + blk, BF16),
            vm((CBLK,) + blk, BF16),
            vm((zslots,) + blk, F32),
            vm((zslots * pieces, padded, BLK), BF16),
            vm((NG, 2, padded, BLK), BF16),
            vm((2, 8, 128), F32),
            vm((8, 8, 128), F32),
            vm((rest_n, 8, 128), F32),
        ] + [pltpu.SemaphoreType.DMA((n,)) for n in sems],
        compiler_params=pltpu.CompilerParams(
            collective_id=0, has_side_effects=True, vmem_limit_bytes=63 * 1024 * 1024
        ),
    )(acts, cotangents)


def solution(mesh):
    groups, width = mesh.shape["grp"], mesh.shape["dp"]
    spec = P(("grp", "dp"), None)
    return jax.shard_map(
        functools.partial(per_device, groups=groups, width=width),
        mesh=mesh, in_specs=(spec, spec), out_specs=spec, check_vma=False,
    )
```

```python
import functools

import jax
import jax.numpy as jnp
from jax import lax
from jax.experimental import pallas as pl
from jax.experimental.pallas import tpu as pltpu
from jax.sharding import PartitionSpec as P

D = 2560
R = 768
BLK = 128
ITERS = 8
NA = D // BLK
NG = R // BLK
QROWS = D // 4
QBLK = QROWS // BLK
CH = 4
PART = BLK // CH
SUB = PART // 2
SROWS = QBLK * SUB
CCOLS = R // 2
CBLK = CCOLS // BLK
PROWS = BLK + 16
A_OWNER = ((0, 1, 0), (0, 1, 1), (1, 2, 0), (1, 2, 1), (0, 2, 0))
G_OWNER = ((0, 2, 1), (1, 1, 0))
MESH = pl.DeviceIdType.MESH
F32 = jnp.float32
BF16 = jnp.bfloat16


def dot(a, b):
    return jnp.dot(a, b, preferred_element_type=F32)


def dot_t(a, b):
    return lax.dot_general(a, b, (((0,), (0,)), ((), ())), preferred_element_type=F32)


def split(a):
    hi = a.astype(BF16)
    return hi, (a - hi.astype(F32)).astype(BF16)


def dot3(a, b):
    ah, al = split(a)
    bh, bl = split(b)
    both = dot(
        jnp.concatenate([ah, al], axis=1),
        jnp.concatenate(
            [jnp.concatenate([bh, bl], axis=1), jnp.concatenate([bh, jnp.zeros_like(bh)], axis=1)],
            axis=0,
        ),
    )
    return both[:, :BLK] + both[:, BLK:]


def kernel(
    groups, width, total, rows,
    x_hbm, g_hbm, out_ref,
    x_ref, g_ref, xt, fpart, f1recv, fzsend, fzrecv, f2send, f2recv,
    m1send, m1recv, mown, masend, m2a, mbsend, m2b,
    zsend, zrecv, state, inv_own, inv_a, inv_g, nat, fin_send, fin_recv, qsend, qrecv,
    in_sem,
    f1_ss, f1_rs, fz_ss, fz_rs, f2_ss, f2_rs, m1_ss, m1_rs, ma_ss, ma_rs,
    mb_ss, mb_rs, z_ss, z_rs, inv_ss, inv_rs, gz_ss, gp_ss, g_rs, fin_ss, fin_rs, q_ss, q_rs,
):
    devices = groups * width
    rest_n = devices // 8
    half_n = devices // 2
    zslots = zsend.shape[1]
    pieces = fin_send.shape[0] // zslots
    dp_rest = width // 4
    gi = lax.axis_index("grp")
    di = lax.axis_index("dp")
    me = gi * width + di
    core = lax.rem(di, 2)
    x = lax.rem(lax.div(di, 2), 2)
    y = lax.rem(gi, 2)
    q = 2 * y + x
    rest = lax.div(gi, 2) * dp_rest + lax.div(di, 4)

    def at(yy, xx, zz, cc):
        return (
            lax.div(zz, dp_rest) * 2 + yy,
            lax.rem(zz, dp_rest) * 4 + xx * 2 + cc,
        )

    def linear(d):
        return (lax.div(d, width), lax.rem(d, width))

    def rcopy(src, dst, ss, rs, dev):
        return pltpu.make_async_remote_copy(
            src_ref=src, dst_ref=dst, send_sem=ss, recv_sem=rs,
            device_id=dev, device_id_type=MESH,
        )

    g_in = pltpu.make_async_copy(g_hbm, g_ref, in_sem.at[4])
    g_in.start()
    x_in = []
    for i in range(4):
        cols = pl.ds(i * QROWS, QROWS)
        x_in.append(pltpu.make_async_copy(x_hbm.at[:, cols], x_ref.at[:, cols], in_sem.at[i]))
        x_in[i].start()

    barrier = pltpu.get_barrier_semaphore()

    def greet(dev):
        pl.semaphore_signal(barrier, inc=1, device_id=dev, device_id_type=MESH)

    greet(at(y, x, rest, 1 - core))
    for yy, xx in ((y, 1 - x), (1 - y, x), (1 - y, 1 - x)):
        greet(at(yy, xx, rest, core))

    @pl.loop(0, rest_n)
    def _(z):
        @pl.when(z != rest)
        def _():
            greet(at(y, x, z, core))

    zero = jnp.zeros((BLK, BLK), BF16)
    g_in.wait()
    g_other = g_ref[:, pl.ds(pl.multiple_of((1 - core) * CCOLS, BLK), CCOLS)]
    g_mine = g_ref[:, pl.ds(pl.multiple_of(core * CCOLS, BLK), CCOLS)]
    for i in range(QBLK * CBLK, zslots * rest_n):
        for k in range(CH):
            zsend[k, i // zslots, i % zslots] = zero[:PART]

    def scatter(ref, yq, xq, t, value):
        for k in range(CH):
            for h in range(2):
                major, minor = (xq, yq) if h == 0 else (yq, xq)
                start = k * PART + h * SUB
                ref[k, h, major, minor, t * SUB:(t + 1) * SUB, :] = value[start:start + SUB]

    if zslots * rest_n > QBLK * CBLK:
        @pl.when(rest * zslots >= QBLK * CBLK)
        def _():
            inv_a[QBLK - 1] = zero

    row = lax.broadcasted_iota(jnp.int32, (BLK, BLK), 0)
    col = lax.broadcasted_iota(jnp.int32, (BLK, BLK), 1)
    eye = (row == col).astype(F32)

    def pack(ref, first, second):
        ref[:BLK, :] = jnp.where(col >= row, first, second).astype(BF16)
        diag = jnp.sum(second * eye, axis=0, keepdims=True)
        ref[BLK:, :] = jnp.broadcast_to(diag, (PROWS - BLK, BLK)).astype(BF16)

    def gram(c):
        gb = g_ref[:, c * BLK:(c + 1) * BLK]
        return dot_t(gb, gb)

    for qq in range(NG - 4):
        last = gram(4 + qq)
        pack(fpart.at[1, qq, 0], last, last)
    for qq in range(NG - 4, 4):
        fpart[1, qq, 0] = jnp.zeros((PROWS, BLK), BF16)

    held = {}
    for part in range(4):
        x_in[part].wait()
        for b in range(part * QBLK, (part + 1) * QBLK):
            yq, xq, t = b // (2 * QBLK), b % 2, b % (2 * QBLK) // 2
            qq = 2 * yq + xq
            xb = x_ref[:, b * BLK:(b + 1) * BLK]
            xbt = xb.T
            xt[b] = xbt
            held[t] = held.get(t, {})
            held[t][qq] = dot(xbt, xb)
            if t == 1:
                pack(fpart.at[0, qq, 0], held[0][qq], held[1][qq])
            elif t == 3:
                pack(fpart.at[1, qq, 1], held[2][qq], held[3][qq])
            elif t == 4:
                pack(fpart.at[0, qq, 1], held[4][qq], gram(qq))
    for b in range(NA):
        yq, xq, t = b // (2 * QBLK), b % 2, b % (2 * QBLK) // 2
        scatter(m1send, yq, xq, t, dot(xt[b], g_other).astype(BF16))

    pl.semaphore_wait(barrier, rest_n + 3)
    other = at(y, x, rest, 1 - core)
    at_x = at(y, 1 - x, rest, core)
    at_y = at(1 - y, x, rest, core)
    f1 = rcopy(fpart.at[1 - core], f1recv, f1_ss.at[0], f1_rs.at[0], other)
    m1 = [rcopy(m1send.at[k], m1recv.at[k], m1_ss.at[k], m1_rs.at[k], other) for k in range(CH)]

    def stage_own(part):
        for b in range(part * QBLK, (part + 1) * QBLK):
            yq, xq, t = b // (2 * QBLK), b % 2, b % (2 * QBLK) // 2
            scatter(mown, yq, xq, t, dot(xt[b], g_mine))

    def summed(k, h, major, minor):
        return mown[k, h, major, minor] + m1recv[k, h, major, minor].astype(F32)

    side = (x, y)
    near = (at_x, at_y)
    ma, mb = {}, {}

    def stage_a(k):
        m1[k].wait_recv()
        for h in range(2):
            for minor in range(2):
                masend[k, h, minor] = summed(k, h, 1 - side[h], minor).astype(BF16)
            ma[k, h] = rcopy(
                masend.at[k, h], m2a.at[k, h], ma_ss.at[2 * k + h], ma_rs.at[2 * k + h], near[h]
            )
            ma[k, h].start()

    def stage_b(k):
        for h in range(2):
            ma[k, h].wait_recv()
            minor = 1 - side[1 - h]
            mbsend[k, h] = (
                summed(k, h, side[h], minor) + m2a[k, h, minor].astype(F32)
            ).astype(BF16)
            mb[k, h] = rcopy(
                mbsend.at[k, h], m2b.at[k, h], mb_ss.at[2 * k + h], mb_rs.at[2 * k + h], near[1 - h]
            )
            mb[k, h].start()

    def z_copy(k, dst, src):
        return rcopy(
            zsend.at[k, dst], zrecv.at[k, src],
            z_ss.at[k * rest_n + dst], z_rs.at[k * rest_n + src], at(y, x, dst, core),
        )

    def stage_z(k):
        for h in range(2):
            mb[k, h].wait_recv()
            minor = side[1 - h]
            value = (
                summed(k, h, side[h], minor) + m2a[k, h, minor].astype(F32) + m2b[k, h].astype(F32)
            ) * (1.0 / total)
            value = value.astype(BF16)
            for i in range(QBLK * CBLK):
                t, c = divmod(i, CBLK)
                zsend[k, i // zslots, i % zslots, h * SUB:(h + 1) * SUB, :] = (
                    value[t * SUB:(t + 1) * SUB, c * BLK:(c + 1) * BLK]
                )

        @pl.loop(0, rest_n)
        def _(z):
            @pl.when(z != rest)
            def _():
                z_copy(k, z, rest).start()

        zrecv[k, rest] = zsend[k, rest]

    def f1_sum(qq, s):
        return fpart[core, qq, s].astype(F32) + f1recv[qq, s].astype(F32)

    chips = [(y, 1 - x), (1 - y, x), (1 - y, 1 - x)]

    def f2_copy(k, s):
        yy, xx = chips[k]
        i = 2 * k + s
        return rcopy(f2send.at[k, s], f2recv.at[k, s], f2_ss.at[i], f2_rs.at[i], at(yy, xx, rest, core))

    def fz_copy(s, src, n):
        return rcopy(
            fzsend.at[s, pl.ds(0, n)], fzrecv.at[src, pl.ds(0, n)], fz_ss.at[s], fz_rs.at[src],
            at(y, x, s + 1, core),
        )

    def with_count(here, s, body):
        late = core if s is None else core * (1 - s)
        if s is None:
            late = core * (2 - rest)

        @pl.when(jnp.logical_and(here, late == 1))
        def _():
            body(NG - 4)

        @pl.when(jnp.logical_and(here, late != 1))
        def _():
            body(4)

    def stage_f1():
        f1.wait_recv()
        for s in range(2):
            for qq in range(4):
                fzsend[s, qq] = f1_sum(qq, s).astype(BF16)
            with_count(rest != s + 1, s, lambda n: fz_copy(s, rest, n).start())

            @pl.when(rest == s + 1)
            def _():
                fzrecv[s + 1] = fzsend[s]

    hub = jnp.logical_or(rest == 1, rest == 2)

    def column_sum(qq):
        f = fzrecv[0, qq].astype(F32)
        for z in range(1, rest_n):
            f = f + fzrecv[z, qq].astype(F32)
        return f

    def f2_copy(k):
        yy, xx = chips[k]
        return rcopy(f2send.at[k], f2recv.at[k], f2_ss.at[k], f2_rs.at[k], at(yy, xx, rest, core))

    def each_f2(body):
        for k, (yy, xx) in enumerate(chips):
            @pl.when(jnp.logical_or(
                rest == 2, jnp.logical_and(rest == 1, jnp.logical_or(core == 0, yy == 0))
            ))
            def _():
                body(k, 2 * yy + xx)

    def send_f2(k, qq):
        f2send[k] = column_sum(qq).astype(BF16)
        f2_copy(k).start()

    def stage_f2():
        def wait(n):
            @pl.loop(0, rest_n)
            def _(z):
                @pl.when(z != rest)
                def _():
                    fz_copy(0, z, n).wait_recv()

        with_count(hub, None, wait)
        each_f2(send_f2)

    is_owner = jnp.logical_or(
        rest == 2, jnp.logical_and(rest == 1, jnp.logical_or(core == 0, y == 0))
    )

    def advance(n):
        pairs = [(state[i, 0], state[i, 1]) for i in range(2)]
        for _ in range(n):
            done = []
            for power, approx in pairs:
                both = dot3(jnp.concatenate([power, approx], axis=0), power)
                done.append((both[:BLK], approx + both[BLK:]))
            pairs = done
        return pairs

    def stage_f3():
        @pl.when(is_owner)
        def _():
            packed = column_sum(q)
            for k in range(3):
                f2_copy(k).wait_recv()
                packed = packed + f2recv[k].astype(F32)
            packed = packed * (1.0 / total)
            half = packed[:BLK]
            flip = half.T
            first = jnp.where(col >= row, half, flip)
            second = jnp.where(col > row, flip, jnp.where(col < row, half, packed[BLK:BLK + 1]))
            for i, factor in enumerate((first, second)):
                trace = jnp.sum(jnp.sum(factor * eye, axis=1, keepdims=True), axis=0, keepdims=True)
                damped = factor + (0.1 * (trace / BLK + 1e-06)) * eye
                peak = jnp.max(jnp.sum(jnp.abs(damped), axis=1, keepdims=True), axis=0, keepdims=True)
                scale = 1.0 / peak
                power = eye - scale * damped
                state[i, 1] = scale * (eye + power)
                state[i, 0] = dot3(power, power)

    def stage_newton(n, last):
        @pl.when(is_owner)
        def _():
            for i, (power, approx) in enumerate(advance(n)):
                if last:
                    inv_own[i] = (approx + dot3(approx, power)).astype(BF16)
                else:
                    state[i, 0] = power
                    state[i, 1] = approx

    def owned(owner):
        return jnp.logical_and(core == owner[0], rest == owner[1])

    def needs(t):
        return range(t * CBLK // zslots, (t * CBLK + CBLK - 1) // zslots + 1)

    a_sends = []
    for t in range(QBLK):
        for z in needs(t):
            for cc in range(2):
                if (cc, z) != A_OWNER[t][:2]:
                    a_sends.append((t, z, cc))

    def a_copy(i):
        t, z, cc = a_sends[i]
        return rcopy(inv_own.at[A_OWNER[t][2]], inv_a.at[t], inv_ss.at[i], inv_rs.at[t], at(y, x, z, cc))

    def g_half(e):
        return lax.div(q + 4 * e, CBLK)

    def gz_copy(e, z):
        return rcopy(
            inv_own.at[G_OWNER[e][2]], inv_g.at[lax.rem(q + 4 * e, CBLK)], gz_ss.at[e * rest_n + z],
            g_rs.at[lax.rem(q + 4 * e, CBLK)], at(y, x, z, g_half(e)),
        )

    def each_gz(body):
        for e in range(2):
            @pl.when(owned(G_OWNER[e]) if e == 0 else jnp.logical_and(owned(G_OWNER[e]), q < NG - 4))
            def _():
                @pl.loop(0, rest_n)
                def _(z):
                    @pl.when(jnp.logical_or(z != rest, g_half(e) != core))
                    def _():
                        body(e, z)

    def stage_inv():
        for i, (t, z, cc) in enumerate(a_sends):
            @pl.when(owned(A_OWNER[t]))
            def _():
                a_copy(i).start()
        each_gz(lambda e, z: gz_copy(e, z).start())
        for t in range(QBLK):
            if A_OWNER[t][1] in needs(t):
                @pl.when(owned(A_OWNER[t]))
                def _():
                    inv_a[t] = inv_own[A_OWNER[t][2]]

    def g_home(j):
        return lax.rem(core * CBLK + j, 4)

    def g_owned(j):
        late = core * CBLK + j >= 4
        return jnp.logical_or(
            jnp.logical_and(late, owned(G_OWNER[1])),
            jnp.logical_and(jnp.logical_not(late), owned(G_OWNER[0])),
        )

    def gp_copy(j, k):
        yy, xx = chips[k]
        return rcopy(inv_g.at[j], inv_g.at[j], gp_ss.at[3 * j + k], g_rs.at[j], at(yy, xx, rest, core))

    def stage_relay():
        for j in range(CBLK):
            @pl.when(q == g_home(j))
            def _():
                @pl.when(g_owned(j))
                def _():
                    inv_g[j] = inv_own[1 - core]

                @pl.when(jnp.logical_not(g_owned(j)))
                def _():
                    gp_copy(j, 0).wait_recv()

                for k in range(3):
                    gp_copy(j, k).start()

    f1.start()
    m1[0].start()
    stage_own(0)
    stage_own(1)
    m1[1].start()
    stage_own(2)
    stage_own(3)
    stage_f1()
    stage_a(0)
    m1[2].start()
    stage_a(1)
    m1[3].start()
    stage_b(0)
    stage_a(2)
    stage_f2()
    stage_b(1)
    stage_z(0)
    stage_a(3)
    stage_f3()
    stage_newton(3, False)
    stage_b(2)
    stage_newton(3, True)
    stage_inv()
    stage_z(1)
    stage_b(3)
    stage_z(2)
    stage_relay()
    stage_z(3)

    for j in range(CBLK):
        @pl.when(q != g_home(j))
        def _():
            gp_copy(j, 0).wait_recv()
    for t in range(QBLK):
        @pl.when(jnp.logical_and(
            jnp.logical_and(rest >= needs(t)[0], rest <= needs(t)[-1]),
            jnp.logical_not(owned(A_OWNER[t])),
        ))
        def _():
            rcopy(inv_own.at[0], inv_a.at[t], inv_ss.at[0], inv_rs.at[t], other).wait_recv()

    @pl.loop(0, rest_n)
    def _(z):
        @pl.when(z != rest)
        def _():
            for k in range(CH):
                z_copy(k, 0, z).wait_recv()

    square = jnp.zeros((1, 1), F32)
    for k in range(zslots):
        tile = rest * zslots + k
        m = jnp.concatenate(
            [sum(zrecv[j, z, k].astype(F32) for z in range(rest_n)) for j in range(CH)], axis=0
        )
        left = dot_t(inv_a[jnp.minimum(lax.div(tile, CBLK), QBLK - 1)], m.astype(BF16))
        hi, lo = split(left)
        ginv = inv_g[lax.rem(tile, CBLK)]
        part = dot(hi, ginv) + dot(lo, ginv)
        nat[k] = part
        square = square + jnp.sum(
            jnp.sum(part * part, axis=0, keepdims=True), axis=1, keepdims=True
        )
    qsend[...] = jnp.broadcast_to(square, (1, 128))

    def q_copy(p):
        return rcopy(qsend, qrecv.at[me], q_ss.at[0], q_rs.at[0], linear(p))

    rest_of = qrecv.at[pl.ds(0, devices - 1)]
    q_all = rcopy(rest_of, rest_of, q_ss.at[0], q_rs.at[0], other)

    def others(n, mine, body):
        @pl.loop(0, n)
        def _(p):
            @pl.when(p != mine)
            def _():
                body(p)

    others(devices, me, lambda p: q_copy(p).start())
    qrecv[me] = qsend[...]

    def each_piece(body):
        for xx in range(2):
            for i in range(QBLK * CBLK):
                t, c = divmod(i, CBLK)
                top = (2 * t + xx) * BLK

                @pl.when(jnp.logical_and(x == xx, rest == i // zslots))
                def _():
                    first = top // rows
                    for k in range(first, (top + BLK + rows - 1) // rows):
                        lo, hi = max(top, k * rows), min(top + BLK, (k + 1) * rows)
                        late = 0 if lo == k * rows else 1
                        body(i % zslots, c, k, lo - k * rows, lo - top, hi - lo, late,
                             i % zslots * pieces + k - first)

    def fin_copy(j, c, late, k):
        return rcopy(
            fin_send.at[j], fin_recv.at[core * CBLK + c, late], fin_ss.at[j],
            fin_rs.at[2 * (core * CBLK + c) + late], linear(y * half_n + k),
        )

    def send_piece(slot_k, c, k, above, start, count, late, j):
        parts = [nat[slot_k, start:start + count, :]]
        if above:
            parts.insert(0, jnp.zeros((above, BLK), F32))
        tail = fin_send.shape[1] - above - count
        if tail:
            parts.append(jnp.zeros((tail, BLK), F32))
        fin_send[j] = (jnp.concatenate(parts, axis=0) if len(parts) > 1 else parts[0]).astype(BF16)

        @pl.when(y * half_n + k != me)
        def _():
            fin_copy(j, c, late, k).start()

        @pl.when(y * half_n + k == me)
        def _():
            fin_recv[core * CBLK + c, late] = fin_send[j]

    each_piece(send_piece)

    k_me = lax.rem(me, half_n)
    t_me = lax.div(k_me * rows, BLK)
    straddles = lax.div(k_me * rows + rows - 1, BLK) > t_me
    mine_here = lax.div(me, half_n) == y
    for late in range(2):
        for c in range(NG):
            from_me = jnp.logical_and(
                jnp.logical_and(mine_here, core == c // CBLK),
                jnp.logical_and(
                    lax.rem(t_me + late, 2) == x,
                    lax.div(CBLK * lax.div(t_me + late, 2) + c % CBLK, zslots) == rest,
                ),
            )
            incoming = jnp.logical_not(from_me)
            if late:
                incoming = jnp.logical_and(straddles, incoming)

                @pl.when(jnp.logical_not(straddles))
                def _():
                    fin_recv[c, 1] = jnp.zeros(fin_recv.shape[2:], BF16)

            @pl.when(incoming)
            def _():
                pltpu.make_async_remote_copy(
                    src_ref=fin_send.at[0], dst_ref=fin_recv.at[c, late], send_sem=fin_ss.at[0],
                    recv_sem=fin_rs.at[2 * c + late], device_id=other, device_id_type=MESH,
                ).wait_recv()

    q_all.wait_recv()
    quad = jnp.sum(qrecv[...], axis=0)[:1, :1] / (D * R)
    factor_out = lax.rsqrt(quad + 1e-06)
    for c in range(NG):
        natural = fin_recv[c, 0].astype(F32) + fin_recv[c, 1].astype(F32)
        out_ref[:, c * BLK:(c + 1) * BLK] = natural[:rows, :] * factor_out

    f1.wait_send()
    for cp in m1 + list(ma.values()) + list(mb.values()):
        cp.wait_send()
    for s in range(2):
        with_count(rest != s + 1, s, lambda n: fz_copy(s, rest, n).wait_send())
    each_f2(lambda k, qq: f2_copy(k).wait_send())
    for i, (t, z, cc) in enumerate(a_sends):
        @pl.when(owned(A_OWNER[t]))
        def _():
            a_copy(i).wait_send()
    each_gz(lambda e, z: gz_copy(e, z).wait_send())
    for j in range(CBLK):
        @pl.when(q == g_home(j))
        def _():
            for k in range(3):
                gp_copy(j, k).wait_send()

    for k in range(CH):
        others(rest_n, rest, lambda z: z_copy(k, z, 0).wait_send())
    q_all.wait_send()

    def wait_piece(slot_k, c, k, above, start, count, late, j):
        @pl.when(y * half_n + k != me)
        def _():
            fin_copy(j, c, late, k).wait_send()

    each_piece(wait_piece)


def per_device(acts, cotangents, groups, width):
    tokens = acts.shape[0]
    devices = groups * width
    rest_n = devices // 8
    rows = D // devices
    padded = (rows + 15) // 16 * 16
    blk = (BLK, BLK)
    zslots = (QBLK * CBLK + rest_n - 1) // rest_n
    pieces = max(
        ((t + 1) * BLK + rows - 1) // rows - t * BLK // rows for t in range(2 * QBLK)
    )
    sems = [5, 1, 1, 2, rest_n, 3, 3, CH, CH, 2 * CH, 2 * CH, 2 * CH, 2 * CH,
            CH * rest_n, CH * rest_n, 2 * CBLK * QBLK, QBLK,
            2 * rest_n, 3 * CBLK, CBLK, zslots * pieces, 2 * NG, 1, 1]
    vm = pltpu.VMEM
    return pl.pallas_call(
        functools.partial(kernel, groups, width, tokens * devices, rows),
        out_shape=jax.ShapeDtypeStruct((rows, R), F32),
        in_specs=[pl.BlockSpec(memory_space=pl.ANY)] * 2,
        out_specs=pl.BlockSpec(memory_space=pltpu.VMEM),
        scratch_shapes=[
            vm((tokens, D), BF16),
            vm((tokens, R), BF16),
            vm((NA, BLK, tokens), BF16),
            vm((2, 4, 2, PROWS, BLK), BF16),
            vm((4, 2, PROWS, BLK), BF16),
            vm((2, 4, PROWS, BLK), BF16),
            vm((rest_n, 4, PROWS, BLK), BF16),
            vm((3, PROWS, BLK), BF16),
            vm((3, PROWS, BLK), BF16),
            vm((CH, 2, 2, 2, SROWS, CCOLS), BF16),
            vm((CH, 2, 2, 2, SROWS, CCOLS), BF16),
            vm((CH, 2, 2, 2, SROWS, CCOLS), F32),
            vm((CH, 2, 2, SROWS, CCOLS), BF16),
            vm((CH, 2, 2, SROWS, CCOLS), BF16),
            vm((CH, 2, SROWS, CCOLS), BF16),
            vm((CH, 2, SROWS, CCOLS), BF16),
            vm((CH, rest_n, zslots, PART, BLK), BF16),
            vm((CH, rest_n, zslots, PART, BLK), BF16),
            vm((2, 2) + blk, F32),
            vm((2,) + blk, BF16),
            vm((QBLK,) + blk, BF16),
            vm((CBLK,) + blk, BF16),
            vm((zslots,) + blk, F32),
            vm((zslots * pieces, padded, BLK), BF16),
            vm((NG, 2, padded, BLK), BF16),
            vm((1, 128), F32),
            vm((devices, 1, 128), F32),
        ] + [pltpu.SemaphoreType.DMA((n,)) for n in sems],
        compiler_params=pltpu.CompilerParams(
            collective_id=0, has_side_effects=True, vmem_limit_bytes=63 * 1024 * 1024
        ),
    )(acts, cotangents)


def solution(mesh):
    groups, width = mesh.shape["grp"], mesh.shape["dp"]
    spec = P(("grp", "dp"), None)
    return jax.shard_map(
        functools.partial(per_device, groups=groups, width=width),
        mesh=mesh, in_specs=(spec, spec), out_specs=spec, check_vma=False,
    )
```

```python
import functools

import jax
import jax.numpy as jnp
from jax import lax
from jax.experimental import pallas as pl
from jax.experimental.pallas import tpu as pltpu
from jax.sharding import PartitionSpec as P

D = 2560
R = 768
BLK = 128
ITERS = 8
NA = D // BLK
NG = R // BLK
QROWS = D // 4
QBLK = QROWS // BLK
CH = 4
PART = BLK // CH
SUB = PART // 2
SROWS = QBLK * SUB
CCOLS = R // 2
CBLK = CCOLS // BLK
PROWS = BLK + 16
A_OWNER = ((0, 1, 0), (0, 1, 1), (1, 2, 0), (1, 2, 1), (0, 2, 0))
G_OWNER = ((0, 2, 1), (1, 1, 0))
MESH = pl.DeviceIdType.MESH
F32 = jnp.float32
BF16 = jnp.bfloat16


def dot(a, b):
    return jnp.dot(a, b, preferred_element_type=F32)


def dot_t(a, b):
    return lax.dot_general(a, b, (((0,), (0,)), ((), ())), preferred_element_type=F32)


def split(a):
    hi = a.astype(BF16)
    return hi, (a - hi.astype(F32)).astype(BF16)


def dot3(a, b):
    ah, al = split(a)
    bh, bl = split(b)
    both = dot(
        jnp.concatenate([ah, al], axis=1),
        jnp.concatenate(
            [jnp.concatenate([bh, bl], axis=1), jnp.concatenate([bh, jnp.zeros_like(bh)], axis=1)],
            axis=0,
        ),
    )
    return both[:, :BLK] + both[:, BLK:]


def kernel(
    groups, width, total, rows,
    x_hbm, g_hbm, out_ref,
    x_ref, g_ref, xt, fpart, f1recv, fzsend, fzrecv, f2send, f2recv,
    m1send, m1recv, mown, masend, m2a, mbsend, m2b,
    zsend, zrecv, state, inv_own, inv_a, inv_g, nat, fin_send, fin_recv, qsend, qrecv,
    know, in_sem,
    f1_ss, f1_rs, fz_ss, fz_rs, f2_ss, f2_rs, m1_ss, m1_rs, ma_ss, ma_rs,
    mb_ss, mb_rs, z_ss, z_rs, inv_ss, inv_rs, gz_ss, gp_ss, g_rs, fin_ss, fin_rs, q_ss, q_rs,
):
    devices = groups * width
    rest_n = devices // 8
    half_n = devices // 2
    zslots = zsend.shape[1]
    pieces = fin_send.shape[0] // zslots
    dp_rest = width // 4
    gi = lax.axis_index("grp")
    di = lax.axis_index("dp")
    me = gi * width + di
    core = lax.rem(di, 2)
    x = lax.rem(lax.div(di, 2), 2)
    y = lax.rem(gi, 2)
    q = 2 * y + x
    rest = lax.div(gi, 2) * dp_rest + lax.div(di, 4)

    def at(yy, xx, zz, cc):
        return (
            lax.div(zz, dp_rest) * 2 + yy,
            lax.rem(zz, dp_rest) * 4 + xx * 2 + cc,
        )

    def linear(d):
        return (lax.div(d, width), lax.rem(d, width))

    def rcopy(src, dst, ss, rs, dev):
        return pltpu.make_async_remote_copy(
            src_ref=src, dst_ref=dst, send_sem=ss, recv_sem=rs,
            device_id=dev, device_id_type=MESH,
        )

    g_in = pltpu.make_async_copy(g_hbm, g_ref, in_sem.at[4])
    g_in.start()
    x_in = []
    for i in range(4):
        cols = pl.ds(i * QROWS, QROWS)
        x_in.append(pltpu.make_async_copy(x_hbm.at[:, cols], x_ref.at[:, cols], in_sem.at[i]))
        x_in[i].start()

    barrier = pltpu.get_barrier_semaphore()

    def greet(dev):
        pl.semaphore_signal(barrier, inc=1, device_id=dev, device_id_type=MESH)

    greet(at(y, x, rest, 1 - core))
    greet(at(y, 1 - x, rest, core))
    greet(at(1 - y, x, rest, core))

    def near_z(reach, body):
        @pl.when(rest >= reach)
        def _():
            body(rest - reach)

        @pl.when(rest + reach < rest_n)
        def _():
            body(rest + reach)

    def sides(reach):
        return (rest >= reach).astype(jnp.int32) + (rest + reach < rest_n).astype(jnp.int32)

    near_z(1, lambda z: greet(at(y, x, z, core)))
    rounds = (rest_n - 2).bit_length()
    hub_rounds = (max(rest_n - 3, 1)).bit_length()

    def tell(r):
        near_z(1 << r, lambda z: pl.semaphore_signal(
            know.at[r], inc=1, device_id=at(y, x, z, core), device_id_type=MESH
        ))

    def hear(first, last):
        for r in range(first, last):
            pl.semaphore_wait(know.at[r], sides(1 << r))
            if r + 1 < rounds:
                tell(r + 1)

    zero = jnp.zeros((BLK, BLK), BF16)
    g_in.wait()
    g_other = g_ref[:, pl.ds(pl.multiple_of((1 - core) * CCOLS, BLK), CCOLS)]
    g_mine = g_ref[:, pl.ds(pl.multiple_of(core * CCOLS, BLK), CCOLS)]
    for i in range(QBLK * CBLK, zslots * rest_n):
        for k in range(CH):
            zsend[k, i // zslots, i % zslots] = zero[:PART]

    def scatter(ref, yq, xq, t, value):
        for k in range(CH):
            for h in range(2):
                major, minor = (xq, yq) if h == 0 else (yq, xq)
                start = k * PART + h * SUB
                ref[k, h, major, minor, t * SUB:(t + 1) * SUB, :] = value[start:start + SUB]

    if zslots * rest_n > QBLK * CBLK:
        @pl.when(rest * zslots >= QBLK * CBLK)
        def _():
            inv_a[QBLK - 1] = zero

    row = lax.broadcasted_iota(jnp.int32, (BLK, BLK), 0)
    col = lax.broadcasted_iota(jnp.int32, (BLK, BLK), 1)
    eye = (row == col).astype(F32)

    def pack(ref, first, second):
        ref[:BLK, :] = jnp.where(col >= row, first, second).astype(BF16)
        diag = jnp.sum(second * eye, axis=0, keepdims=True)
        ref[BLK:, :] = jnp.broadcast_to(diag, (PROWS - BLK, BLK)).astype(BF16)

    def gram(c):
        gb = g_ref[:, c * BLK:(c + 1) * BLK]
        return dot_t(gb, gb)

    for qq in range(NG - 4):
        last = gram(4 + qq)
        pack(fpart.at[1, qq, 0], last, last)
    for qq in range(NG - 4, 4):
        fpart[1, qq, 0] = jnp.zeros((PROWS, BLK), BF16)

    held = {}
    for part in range(4):
        x_in[part].wait()
        for b in range(part * QBLK, (part + 1) * QBLK):
            yq, xq, t = b // (2 * QBLK), b % 2, b % (2 * QBLK) // 2
            qq = 2 * yq + xq
            xb = x_ref[:, b * BLK:(b + 1) * BLK]
            xbt = xb.T
            xt[b] = xbt
            held[t] = held.get(t, {})
            held[t][qq] = dot(xbt, xb)
            if t == 1:
                pack(fpart.at[0, qq, 0], held[0][qq], held[1][qq])
            elif t == 3:
                pack(fpart.at[1, qq, 1], held[2][qq], held[3][qq])
            elif t == 4:
                pack(fpart.at[0, qq, 1], held[4][qq], gram(qq))
    for b in range(NA):
        yq, xq, t = b // (2 * QBLK), b % 2, b % (2 * QBLK) // 2
        scatter(m1send, yq, xq, t, dot(xt[b], g_other).astype(BF16))

    pl.semaphore_wait(barrier, 3 + sides(1))
    tell(0)
    other = at(y, x, rest, 1 - core)
    at_x = at(y, 1 - x, rest, core)
    at_y = at(1 - y, x, rest, core)
    f1 = rcopy(fpart.at[1 - core], f1recv, f1_ss.at[0], f1_rs.at[0], other)
    m1 = [rcopy(m1send.at[k], m1recv.at[k], m1_ss.at[k], m1_rs.at[k], other) for k in range(CH)]

    def stage_own(part):
        for b in range(part * QBLK, (part + 1) * QBLK):
            yq, xq, t = b // (2 * QBLK), b % 2, b % (2 * QBLK) // 2
            scatter(mown, yq, xq, t, dot(xt[b], g_mine))

    def summed(k, h, major, minor):
        return mown[k, h, major, minor] + m1recv[k, h, major, minor].astype(F32)

    side = (x, y)
    near = (at_x, at_y)
    ma, mb = {}, {}

    def stage_a(k):
        m1[k].wait_recv()
        for h in range(2):
            for minor in range(2):
                masend[k, h, minor] = summed(k, h, 1 - side[h], minor).astype(BF16)
            ma[k, h] = rcopy(
                masend.at[k, h], m2a.at[k, h], ma_ss.at[2 * k + h], ma_rs.at[2 * k + h], near[h]
            )
            ma[k, h].start()

    def stage_b(k):
        for h in range(2):
            ma[k, h].wait_recv()
            minor = 1 - side[1 - h]
            mbsend[k, h] = (
                summed(k, h, side[h], minor) + m2a[k, h, minor].astype(F32)
            ).astype(BF16)
            mb[k, h] = rcopy(
                mbsend.at[k, h], m2b.at[k, h], mb_ss.at[2 * k + h], mb_rs.at[2 * k + h], near[1 - h]
            )
            mb[k, h].start()

    def z_copy(k, dst, src):
        return rcopy(
            zsend.at[k, dst], zrecv.at[k, src],
            z_ss.at[k * rest_n + dst], z_rs.at[k * rest_n + src], at(y, x, dst, core),
        )

    chips = [(y, 1 - x), (1 - y, x), (1 - y, 1 - x)]

    def stage_z(k):
        if k == 0:
            hear(hub_rounds, rounds)
        for h in range(2):
            mb[k, h].wait_recv()
            minor = side[1 - h]
            value = (
                summed(k, h, side[h], minor) + m2a[k, h, minor].astype(F32) + m2b[k, h].astype(F32)
            ) * (1.0 / total)
            value = value.astype(BF16)
            for i in range(QBLK * CBLK):
                t, c = divmod(i, CBLK)
                zsend[k, i // zslots, i % zslots, h * SUB:(h + 1) * SUB, :] = (
                    value[t * SUB:(t + 1) * SUB, c * BLK:(c + 1) * BLK]
                )

        @pl.loop(0, rest_n)
        def _(z):
            @pl.when(z != rest)
            def _():
                z_copy(k, z, rest).start()

        zrecv[k, rest] = zsend[k, rest]

    def f1_sum(qq, s):
        return fpart[core, qq, s].astype(F32) + f1recv[qq, s].astype(F32)


    def f2_copy(k, s):
        yy, xx = chips[k]
        i = 2 * k + s
        return rcopy(f2send.at[k, s], f2recv.at[k, s], f2_ss.at[i], f2_rs.at[i], at(yy, xx, rest, core))

    def fz_copy(s, src, n):
        return rcopy(
            fzsend.at[s, pl.ds(0, n)], fzrecv.at[src, pl.ds(0, n)], fz_ss.at[s], fz_rs.at[src],
            at(y, x, s + 1, core),
        )

    def with_count(here, s, body):
        late = core if s is None else core * (1 - s)
        if s is None:
            late = core * (2 - rest)

        @pl.when(jnp.logical_and(here, late == 1))
        def _():
            body(NG - 4)

        @pl.when(jnp.logical_and(here, late != 1))
        def _():
            body(4)

    def stage_f1():
        hear(0, hub_rounds)
        f1.wait_recv()
        for s in range(2):
            for qq in range(4):
                fzsend[s, qq] = f1_sum(qq, s).astype(BF16)
            with_count(rest != s + 1, s, lambda n: fz_copy(s, rest, n).start())

            @pl.when(rest == s + 1)
            def _():
                fzrecv[s + 1] = fzsend[s]

    hub = jnp.logical_or(rest == 1, rest == 2)

    def column_sum(qq):
        f = fzrecv[0, qq].astype(F32)
        for z in range(1, rest_n):
            f = f + fzrecv[z, qq].astype(F32)
        return f

    def f2_copy(k):
        yy, xx = chips[k]
        return rcopy(f2send.at[k], f2recv.at[k], f2_ss.at[k], f2_rs.at[k], at(yy, xx, rest, core))

    def each_f2(body):
        for k, (yy, xx) in enumerate(chips):
            @pl.when(jnp.logical_or(
                rest == 2, jnp.logical_and(rest == 1, jnp.logical_or(core == 0, yy == 0))
            ))
            def _():
                body(k, 2 * yy + xx)

    def send_f2(k, qq):
        f2send[k] = column_sum(qq).astype(BF16)
        f2_copy(k).start()

    def stage_f2():
        def wait(n):
            @pl.loop(0, rest_n)
            def _(z):
                @pl.when(z != rest)
                def _():
                    fz_copy(0, z, n).wait_recv()

        with_count(hub, None, wait)
        each_f2(send_f2)

    is_owner = jnp.logical_or(
        rest == 2, jnp.logical_and(rest == 1, jnp.logical_or(core == 0, y == 0))
    )

    def advance(n):
        pairs = [(state[i, 0], state[i, 1]) for i in range(2)]
        for _ in range(n):
            done = []
            for power, approx in pairs:
                both = dot3(jnp.concatenate([power, approx], axis=0), power)
                done.append((both[:BLK], approx + both[BLK:]))
            pairs = done
        return pairs

    def stage_f3():
        @pl.when(is_owner)
        def _():
            packed = column_sum(q)
            for k in range(3):
                f2_copy(k).wait_recv()
                packed = packed + f2recv[k].astype(F32)
            packed = packed * (1.0 / total)
            half = packed[:BLK]
            flip = half.T
            first = jnp.where(col >= row, half, flip)
            second = jnp.where(col > row, flip, jnp.where(col < row, half, packed[BLK:BLK + 1]))
            for i, factor in enumerate((first, second)):
                trace = jnp.sum(jnp.sum(factor * eye, axis=1, keepdims=True), axis=0, keepdims=True)
                damped = factor + (0.1 * (trace / BLK + 1e-06)) * eye
                peak = jnp.max(jnp.sum(jnp.abs(damped), axis=1, keepdims=True), axis=0, keepdims=True)
                scale = 1.0 / peak
                power = eye - scale * damped
                state[i, 1] = scale * (eye + power)
                state[i, 0] = dot3(power, power)

    def stage_newton(n, last):
        @pl.when(is_owner)
        def _():
            for i, (power, approx) in enumerate(advance(n)):
                if last:
                    inv_own[i] = (approx + dot3(approx, power)).astype(BF16)
                else:
                    state[i, 0] = power
                    state[i, 1] = approx

    def owned(owner):
        return jnp.logical_and(core == owner[0], rest == owner[1])

    def needs(t):
        return range(t * CBLK // zslots, (t * CBLK + CBLK - 1) // zslots + 1)

    a_sends = []
    for t in range(QBLK):
        for z in needs(t):
            for cc in range(2):
                if (cc, z) != A_OWNER[t][:2]:
                    a_sends.append((t, z, cc))

    def a_copy(i):
        t, z, cc = a_sends[i]
        return rcopy(inv_own.at[A_OWNER[t][2]], inv_a.at[t], inv_ss.at[i], inv_rs.at[t], at(y, x, z, cc))

    def g_half(e):
        return lax.div(q + 4 * e, CBLK)

    def gz_copy(e, z):
        return rcopy(
            inv_own.at[G_OWNER[e][2]], inv_g.at[lax.rem(q + 4 * e, CBLK)], gz_ss.at[e * rest_n + z],
            g_rs.at[lax.rem(q + 4 * e, CBLK)], at(y, x, z, g_half(e)),
        )

    def each_gz(body):
        for e in range(2):
            @pl.when(owned(G_OWNER[e]) if e == 0 else jnp.logical_and(owned(G_OWNER[e]), q < NG - 4))
            def _():
                @pl.loop(0, rest_n)
                def _(z):
                    @pl.when(jnp.logical_or(z != rest, g_half(e) != core))
                    def _():
                        body(e, z)

    def stage_inv():
        for i, (t, z, cc) in enumerate(a_sends):
            @pl.when(owned(A_OWNER[t]))
            def _():
                a_copy(i).start()
        each_gz(lambda e, z: gz_copy(e, z).start())
        for t in range(QBLK):
            if A_OWNER[t][1] in needs(t):
                @pl.when(owned(A_OWNER[t]))
                def _():
                    inv_a[t] = inv_own[A_OWNER[t][2]]

    def g_home(j):
        return lax.rem(core * CBLK + j, 4)

    def g_owned(j):
        late = core * CBLK + j >= 4
        return jnp.logical_or(
            jnp.logical_and(late, owned(G_OWNER[1])),
            jnp.logical_and(jnp.logical_not(late), owned(G_OWNER[0])),
        )

    def gp_copy(j, k):
        yy, xx = chips[k]
        return rcopy(inv_g.at[j], inv_g.at[j], gp_ss.at[3 * j + k], g_rs.at[j], at(yy, xx, rest, core))

    def stage_relay():
        for j in range(CBLK):
            @pl.when(q == g_home(j))
            def _():
                @pl.when(g_owned(j))
                def _():
                    inv_g[j] = inv_own[1 - core]

                @pl.when(jnp.logical_not(g_owned(j)))
                def _():
                    gp_copy(j, 0).wait_recv()

                for k in range(3):
                    gp_copy(j, k).start()

    m1[0].start()
    f1.start()
    stage_own(0)
    stage_own(1)
    m1[1].start()
    stage_own(2)
    stage_own(3)
    stage_a(0)
    stage_f1()
    m1[2].start()
    stage_a(1)
    m1[3].start()
    stage_b(0)
    stage_a(2)
    stage_f2()
    stage_b(1)
    stage_a(3)
    stage_z(0)
    stage_f3()
    stage_newton(3, False)
    stage_newton(3, True)
    stage_inv()
    stage_b(2)
    stage_z(1)
    stage_b(3)
    stage_z(2)
    stage_relay()
    stage_z(3)

    for j in range(CBLK):
        @pl.when(q != g_home(j))
        def _():
            gp_copy(j, 0).wait_recv()
    for t in range(QBLK):
        @pl.when(jnp.logical_and(
            jnp.logical_and(rest >= needs(t)[0], rest <= needs(t)[-1]),
            jnp.logical_not(owned(A_OWNER[t])),
        ))
        def _():
            rcopy(inv_own.at[0], inv_a.at[t], inv_ss.at[0], inv_rs.at[t], other).wait_recv()

    @pl.loop(0, rest_n)
    def _(z):
        @pl.when(z != rest)
        def _():
            for k in range(CH):
                z_copy(k, 0, z).wait_recv()

    square = jnp.zeros((1, 1), F32)
    for k in range(zslots):
        tile = rest * zslots + k
        m = jnp.concatenate(
            [sum(zrecv[j, z, k].astype(F32) for z in range(rest_n)) for j in range(CH)], axis=0
        )
        left = dot_t(inv_a[jnp.minimum(lax.div(tile, CBLK), QBLK - 1)], m.astype(BF16))
        hi, lo = split(left)
        ginv = inv_g[lax.rem(tile, CBLK)]
        part = dot(hi, ginv) + dot(lo, ginv)
        nat[k] = part
        square = square + jnp.sum(
            jnp.sum(part * part, axis=0, keepdims=True), axis=1, keepdims=True
        )
    qsend[...] = jnp.broadcast_to(square, (1, 128))

    def q_copy(p):
        return rcopy(qsend, qrecv.at[me], q_ss.at[0], q_rs.at[0], linear(p))

    rest_of = qrecv.at[pl.ds(0, devices - 1)]
    q_all = rcopy(rest_of, rest_of, q_ss.at[0], q_rs.at[0], other)

    def others(n, mine, body):
        @pl.loop(0, n)
        def _(p):
            @pl.when(p != mine)
            def _():
                body(p)

    others(devices, me, lambda p: q_copy(p).start())
    qrecv[me] = qsend[...]

    def each_piece(body):
        for xx in range(2):
            for i in range(QBLK * CBLK):
                t, c = divmod(i, CBLK)
                top = (2 * t + xx) * BLK

                @pl.when(jnp.logical_and(x == xx, rest == i // zslots))
                def _():
                    first = top // rows
                    for k in range(first, (top + BLK + rows - 1) // rows):
                        lo, hi = max(top, k * rows), min(top + BLK, (k + 1) * rows)
                        late = 0 if lo == k * rows else 1
                        body(i % zslots, c, k, lo - k * rows, lo - top, hi - lo, late,
                             i % zslots * pieces + k - first)

    def fin_copy(j, c, late, k):
        return rcopy(
            fin_send.at[j], fin_recv.at[core * CBLK + c, late], fin_ss.at[j],
            fin_rs.at[2 * (core * CBLK + c) + late], linear(y * half_n + k),
        )

    def send_piece(slot_k, c, k, above, start, count, late, j):
        parts = [nat[slot_k, start:start + count, :]]
        if above:
            parts.insert(0, jnp.zeros((above, BLK), F32))
        tail = fin_send.shape[1] - above - count
        if tail:
            parts.append(jnp.zeros((tail, BLK), F32))
        fin_send[j] = (jnp.concatenate(parts, axis=0) if len(parts) > 1 else parts[0]).astype(BF16)

        @pl.when(y * half_n + k != me)
        def _():
            fin_copy(j, c, late, k).start()

        @pl.when(y * half_n + k == me)
        def _():
            fin_recv[core * CBLK + c, late] = fin_send[j]

    each_piece(send_piece)

    k_me = lax.rem(me, half_n)
    t_me = lax.div(k_me * rows, BLK)
    straddles = lax.div(k_me * rows + rows - 1, BLK) > t_me
    mine_here = lax.div(me, half_n) == y
    for late in range(2):
        for c in range(NG):
            from_me = jnp.logical_and(
                jnp.logical_and(mine_here, core == c // CBLK),
                jnp.logical_and(
                    lax.rem(t_me + late, 2) == x,
                    lax.div(CBLK * lax.div(t_me + late, 2) + c % CBLK, zslots) == rest,
                ),
            )
            incoming = jnp.logical_not(from_me)
            if late:
                incoming = jnp.logical_and(straddles, incoming)

                @pl.when(jnp.logical_not(straddles))
                def _():
                    fin_recv[c, 1] = jnp.zeros(fin_recv.shape[2:], BF16)

            @pl.when(incoming)
            def _():
                pltpu.make_async_remote_copy(
                    src_ref=fin_send.at[0], dst_ref=fin_recv.at[c, late], send_sem=fin_ss.at[0],
                    recv_sem=fin_rs.at[2 * c + late], device_id=other, device_id_type=MESH,
                ).wait_recv()

    q_all.wait_recv()
    quad = jnp.sum(qrecv[...], axis=0)[:1, :1] / (D * R)
    factor_out = lax.rsqrt(quad + 1e-06)
    for c in range(NG):
        natural = fin_recv[c, 0].astype(F32) + fin_recv[c, 1].astype(F32)
        out_ref[:, c * BLK:(c + 1) * BLK] = natural[:rows, :] * factor_out

    f1.wait_send()
    for cp in m1 + list(ma.values()) + list(mb.values()):
        cp.wait_send()
    for s in range(2):
        with_count(rest != s + 1, s, lambda n: fz_copy(s, rest, n).wait_send())
    each_f2(lambda k, qq: f2_copy(k).wait_send())
    for i, (t, z, cc) in enumerate(a_sends):
        @pl.when(owned(A_OWNER[t]))
        def _():
            a_copy(i).wait_send()
    each_gz(lambda e, z: gz_copy(e, z).wait_send())
    for j in range(CBLK):
        @pl.when(q == g_home(j))
        def _():
            for k in range(3):
                gp_copy(j, k).wait_send()

    for k in range(CH):
        others(rest_n, rest, lambda z: z_copy(k, z, 0).wait_send())
    q_all.wait_send()

    def wait_piece(slot_k, c, k, above, start, count, late, j):
        @pl.when(y * half_n + k != me)
        def _():
            fin_copy(j, c, late, k).wait_send()

    each_piece(wait_piece)


def per_device(acts, cotangents, groups, width):
    tokens = acts.shape[0]
    devices = groups * width
    rest_n = devices // 8
    rows = D // devices
    padded = (rows + 15) // 16 * 16
    blk = (BLK, BLK)
    zslots = (QBLK * CBLK + rest_n - 1) // rest_n
    pieces = max(
        ((t + 1) * BLK + rows - 1) // rows - t * BLK // rows for t in range(2 * QBLK)
    )
    sems = [5, 1, 1, 2, rest_n, 3, 3, CH, CH, 2 * CH, 2 * CH, 2 * CH, 2 * CH,
            CH * rest_n, CH * rest_n, 2 * CBLK * QBLK, QBLK,
            2 * rest_n, 3 * CBLK, CBLK, zslots * pieces, 2 * NG, 1, 1]
    vm = pltpu.VMEM
    return pl.pallas_call(
        functools.partial(kernel, groups, width, tokens * devices, rows),
        out_shape=jax.ShapeDtypeStruct((rows, R), F32),
        in_specs=[pl.BlockSpec(memory_space=pl.ANY)] * 2,
        out_specs=pl.BlockSpec(memory_space=pltpu.VMEM),
        scratch_shapes=[
            vm((tokens, D), BF16),
            vm((tokens, R), BF16),
            vm((NA, BLK, tokens), BF16),
            vm((2, 4, 2, PROWS, BLK), BF16),
            vm((4, 2, PROWS, BLK), BF16),
            vm((2, 4, PROWS, BLK), BF16),
            vm((rest_n, 4, PROWS, BLK), BF16),
            vm((3, PROWS, BLK), BF16),
            vm((3, PROWS, BLK), BF16),
            vm((CH, 2, 2, 2, SROWS, CCOLS), BF16),
            vm((CH, 2, 2, 2, SROWS, CCOLS), BF16),
            vm((CH, 2, 2, 2, SROWS, CCOLS), F32),
            vm((CH, 2, 2, SROWS, CCOLS), BF16),
            vm((CH, 2, 2, SROWS, CCOLS), BF16),
            vm((CH, 2, SROWS, CCOLS), BF16),
            vm((CH, 2, SROWS, CCOLS), BF16),
            vm((CH, rest_n, zslots, PART, BLK), BF16),
            vm((CH, rest_n, zslots, PART, BLK), BF16),
            vm((2, 2) + blk, F32),
            vm((2,) + blk, BF16),
            vm((QBLK,) + blk, BF16),
            vm((CBLK,) + blk, BF16),
            vm((zslots,) + blk, F32),
            vm((zslots * pieces, padded, BLK), BF16),
            vm((NG, 2, padded, BLK), BF16),
            vm((1, 128), F32),
            vm((devices, 1, 128), F32),
            pltpu.SemaphoreType.REGULAR((8,)),
        ] + [pltpu.SemaphoreType.DMA((n,)) for n in sems],
        compiler_params=pltpu.CompilerParams(
            collective_id=0, has_side_effects=True, vmem_limit_bytes=63 * 1024 * 1024
        ),
    )(acts, cotangents)


def solution(mesh):
    groups, width = mesh.shape["grp"], mesh.shape["dp"]
    spec = P(("grp", "dp"), None)
    return jax.shard_map(
        functools.partial(per_device, groups=groups, width=width),
        mesh=mesh, in_specs=(spec, spec), out_specs=spec, check_vma=False,
    )
```

```python
import functools

import jax
import jax.numpy as jnp
from jax import lax
from jax.experimental import pallas as pl
from jax.experimental.pallas import tpu as pltpu
from jax.sharding import PartitionSpec as P

D = 2560
R = 768
BLK = 128
ITERS = 8
NA = D // BLK
NG = R // BLK
QROWS = D // 4
QBLK = QROWS // BLK
CH = 4
PART = BLK // CH
SUB = PART // 2
SROWS = QBLK * SUB
CCOLS = R // 2
CBLK = CCOLS // BLK
PROWS = BLK + 16
A_OWNER = ((0, 1, 0), (0, 1, 1), (1, 2, 0), (1, 2, 1), (0, 2, 0))
G_OWNER = ((0, 2, 1), (1, 1, 0))
MESH = pl.DeviceIdType.MESH
F32 = jnp.float32
BF16 = jnp.bfloat16


def dot(a, b):
    return jnp.dot(a, b, preferred_element_type=F32)


def dot_t(a, b):
    return lax.dot_general(a, b, (((0,), (0,)), ((), ())), preferred_element_type=F32)


def split(a):
    hi = a.astype(BF16)
    return hi, (a - hi.astype(F32)).astype(BF16)


def dot3(a, b):
    ah, al = split(a)
    bh, bl = split(b)
    both = dot(
        jnp.concatenate([ah, al], axis=1),
        jnp.concatenate(
            [jnp.concatenate([bh, bl], axis=1), jnp.concatenate([bh, jnp.zeros_like(bh)], axis=1)],
            axis=0,
        ),
    )
    return both[:, :BLK] + both[:, BLK:]


def kernel(
    groups, width, total, rows,
    x_hbm, g_hbm, out_ref,
    x_ref, g_ref, xt, fpart, f1recv, fzsend, fzrecv, f2send, f2recv,
    m1send, m1recv, mown, masend, m2a, mbsend, m2b,
    zsend, zrecv, state, inv_own, inv_a, inv_g, nat, fin_send, fin_recv, qsend, qrecv,
    know, in_sem,
    f1_ss, f1_rs, fz_ss, fz_rs, f2_ss, f2_rs, m1_ss, m1_rs, ma_ss, ma_rs,
    mb_ss, mb_rs, z_ss, z_rs, inv_ss, inv_rs, gz_ss, gp_ss, g_rs, fin_ss, fin_rs, q_ss, q_rs,
):
    devices = groups * width
    rest_n = devices // 8
    half_n = devices // 2
    zslots = zsend.shape[1]
    pieces = fin_send.shape[0] // zslots
    dp_rest = width // 4
    gi = lax.axis_index("grp")
    di = lax.axis_index("dp")
    me = gi * width + di
    core = lax.rem(di, 2)
    x = lax.rem(lax.div(di, 2), 2)
    y = lax.rem(gi, 2)
    q = 2 * y + x
    rest = lax.div(gi, 2) * dp_rest + lax.div(di, 4)

    def at(yy, xx, zz, cc):
        return (
            lax.div(zz, dp_rest) * 2 + yy,
            lax.rem(zz, dp_rest) * 4 + xx * 2 + cc,
        )

    def linear(d):
        return (lax.div(d, width), lax.rem(d, width))

    def rcopy(src, dst, ss, rs, dev):
        return pltpu.make_async_remote_copy(
            src_ref=src, dst_ref=dst, send_sem=ss, recv_sem=rs,
            device_id=dev, device_id_type=MESH,
        )

    g_in = pltpu.make_async_copy(g_hbm, g_ref, in_sem.at[4])
    g_in.start()
    x_in = []
    for i in range(4):
        cols = pl.ds(i * QROWS, QROWS)
        x_in.append(pltpu.make_async_copy(x_hbm.at[:, cols], x_ref.at[:, cols], in_sem.at[i]))
        x_in[i].start()

    barrier = pltpu.get_barrier_semaphore()

    def greet(dev):
        pl.semaphore_signal(barrier, inc=1, device_id=dev, device_id_type=MESH)

    greet(at(y, x, rest, 1 - core))
    greet(at(y, 1 - x, rest, core))
    greet(at(1 - y, x, rest, core))

    def near_z(reach, body):
        @pl.when(rest >= reach)
        def _():
            body(rest - reach)

        @pl.when(rest + reach < rest_n)
        def _():
            body(rest + reach)

    def sides(reach):
        return (rest >= reach).astype(jnp.int32) + (rest + reach < rest_n).astype(jnp.int32)

    near_z(1, lambda z: greet(at(y, x, z, core)))
    rounds = (rest_n - 2).bit_length()
    hub_rounds = (max(rest_n - 3, 1)).bit_length()

    def tell(r):
        near_z(1 << r, lambda z: pl.semaphore_signal(
            know.at[r], inc=1, device_id=at(y, x, z, core), device_id_type=MESH
        ))

    def hear(first, last):
        for r in range(first, last):
            pl.semaphore_wait(know.at[r], sides(1 << r))
            if r + 1 < rounds:
                tell(r + 1)

    zero = jnp.zeros((BLK, BLK), BF16)
    g_in.wait()
    g_other = g_ref[:, pl.ds(pl.multiple_of((1 - core) * CCOLS, BLK), CCOLS)]
    g_mine = g_ref[:, pl.ds(pl.multiple_of(core * CCOLS, BLK), CCOLS)]
    for i in range(QBLK * CBLK, zslots * rest_n):
        for k in range(CH):
            zsend[k, i // zslots, i % zslots] = zero[:PART]

    def scatter(ref, yq, xq, t, value):
        for k in range(CH):
            for h in range(2):
                major, minor = (xq, yq) if h == 0 else (yq, xq)
                start = k * PART + h * SUB
                ref[k, h, major, minor, t * SUB:(t + 1) * SUB, :] = value[start:start + SUB]

    if zslots * rest_n > QBLK * CBLK:
        @pl.when(rest * zslots >= QBLK * CBLK)
        def _():
            inv_a[QBLK - 1] = zero

    row = lax.broadcasted_iota(jnp.int32, (BLK, BLK), 0)
    col = lax.broadcasted_iota(jnp.int32, (BLK, BLK), 1)
    eye = (row == col).astype(F32)

    def pack(ref, first, second):
        ref[:BLK, :] = jnp.where(col >= row, first, second).astype(BF16)
        diag = jnp.sum(second * eye, axis=0, keepdims=True)
        ref[BLK:, :] = jnp.broadcast_to(diag, (PROWS - BLK, BLK)).astype(BF16)

    def gram(c):
        gb = g_ref[:, c * BLK:(c + 1) * BLK]
        return dot_t(gb, gb)

    for qq in range(NG - 4):
        last = gram(4 + qq)
        pack(fpart.at[1, qq, 0], last, last)
    for qq in range(NG - 4, 4):
        fpart[1, qq, 0] = jnp.zeros((PROWS, BLK), BF16)

    held = {}
    for part in range(4):
        x_in[part].wait()
        for b in range(part * QBLK, (part + 1) * QBLK):
            yq, xq, t = b // (2 * QBLK), b % 2, b % (2 * QBLK) // 2
            qq = 2 * yq + xq
            xb = x_ref[:, b * BLK:(b + 1) * BLK]
            xbt = xb.T
            xt[b] = xbt
            held[t] = held.get(t, {})
            held[t][qq] = dot(xbt, xb)
            if t == 1:
                pack(fpart.at[0, qq, 0], held[0][qq], held[1][qq])
            elif t == 3:
                pack(fpart.at[1, qq, 1], held[2][qq], held[3][qq])
            elif t == 4:
                pack(fpart.at[0, qq, 1], held[4][qq], gram(qq))
    for b in range(NA):
        yq, xq, t = b // (2 * QBLK), b % 2, b % (2 * QBLK) // 2
        scatter(m1send, yq, xq, t, dot(xt[b], g_other).astype(BF16))

    pl.semaphore_wait(barrier, 3 + sides(1))
    tell(0)
    other = at(y, x, rest, 1 - core)
    at_x = at(y, 1 - x, rest, core)
    at_y = at(1 - y, x, rest, core)
    f1 = rcopy(fpart.at[1 - core], f1recv, f1_ss.at[0], f1_rs.at[0], other)
    m1 = [rcopy(m1send.at[k], m1recv.at[k], m1_ss.at[k], m1_rs.at[k], other) for k in range(CH)]

    def stage_own(part):
        for b in range(part * QBLK, (part + 1) * QBLK):
            yq, xq, t = b // (2 * QBLK), b % 2, b % (2 * QBLK) // 2
            scatter(mown, yq, xq, t, dot(xt[b], g_mine))

    def summed(k, h, major, minor):
        return mown[k, h, major, minor] + m1recv[k, h, major, minor].astype(F32)

    side = (x, y)
    near = (at_x, at_y)
    ma, mb = {}, {}

    def stage_a(k):
        m1[k].wait_recv()
        for h in range(2):
            for minor in range(2):
                masend[k, h, minor] = summed(k, h, 1 - side[h], minor).astype(BF16)
            ma[k, h] = rcopy(
                masend.at[k, h], m2a.at[k, h], ma_ss.at[2 * k + h], ma_rs.at[2 * k + h], near[h]
            )
            ma[k, h].start()

    def stage_b(k):
        for h in range(2):
            ma[k, h].wait_recv()
            minor = 1 - side[1 - h]
            mbsend[k, h] = (
                summed(k, h, side[h], minor) + m2a[k, h, minor].astype(F32)
            ).astype(BF16)
            mb[k, h] = rcopy(
                mbsend.at[k, h], m2b.at[k, h], mb_ss.at[2 * k + h], mb_rs.at[2 * k + h], near[1 - h]
            )
            mb[k, h].start()

    def z_copy(k, dst, src):
        return rcopy(
            zsend.at[k, dst], zrecv.at[k, src],
            z_ss.at[k * rest_n + dst], z_rs.at[k * rest_n + src], at(y, x, dst, core),
        )

    chips = [(y, 1 - x), (1 - y, x), (1 - y, 1 - x)]

    def stage_z(k):
        if k == 0:
            hear(hub_rounds, rounds)
        for h in range(2):
            mb[k, h].wait_recv()
            minor = side[1 - h]
            value = (
                summed(k, h, side[h], minor) + m2a[k, h, minor].astype(F32) + m2b[k, h].astype(F32)
            ) * (1.0 / total)
            value = value.astype(BF16)
            for i in range(QBLK * CBLK):
                t, c = divmod(i, CBLK)
                zsend[k, i // zslots, i % zslots, h * SUB:(h + 1) * SUB, :] = (
                    value[t * SUB:(t + 1) * SUB, c * BLK:(c + 1) * BLK]
                )

        @pl.loop(0, rest_n)
        def _(z):
            @pl.when(z != rest)
            def _():
                z_copy(k, z, rest).start()

        zrecv[k, rest] = zsend[k, rest]

    def f1_sum(qq, s):
        return fpart[core, qq, s].astype(F32) + f1recv[qq, s].astype(F32)


    def f2_copy(k, s):
        yy, xx = chips[k]
        i = 2 * k + s
        return rcopy(f2send.at[k, s], f2recv.at[k, s], f2_ss.at[i], f2_rs.at[i], at(yy, xx, rest, core))

    def fz_copy(s, src, n):
        return rcopy(
            fzsend.at[s, pl.ds(0, n)], fzrecv.at[src, pl.ds(0, n)], fz_ss.at[s], fz_rs.at[src],
            at(y, x, s + 1, core),
        )

    def with_count(here, s, body):
        late = core if s is None else core * (1 - s)
        if s is None:
            late = core * (2 - rest)

        @pl.when(jnp.logical_and(here, late == 1))
        def _():
            body(NG - 4)

        @pl.when(jnp.logical_and(here, late != 1))
        def _():
            body(4)

    def stage_f1():
        hear(0, hub_rounds)
        f1.wait_recv()
        for s in range(2):
            for qq in range(4):
                fzsend[s, qq] = f1_sum(qq, s).astype(BF16)
            with_count(rest != s + 1, s, lambda n: fz_copy(s, rest, n).start())

            @pl.when(rest == s + 1)
            def _():
                fzrecv[s + 1] = fzsend[s]

    hub = jnp.logical_or(rest == 1, rest == 2)

    def column_sum(qq):
        f = fzrecv[0, qq].astype(F32)
        for z in range(1, rest_n):
            f = f + fzrecv[z, qq].astype(F32)
        return f

    def f2_copy(k):
        yy, xx = chips[k]
        return rcopy(f2send.at[k], f2recv.at[k], f2_ss.at[k], f2_rs.at[k], at(yy, xx, rest, core))

    def each_f2(body):
        for k, (yy, xx) in enumerate(chips):
            @pl.when(jnp.logical_or(
                rest == 2, jnp.logical_and(rest == 1, jnp.logical_or(core == 0, yy == 0))
            ))
            def _():
                body(k, 2 * yy + xx)

    def send_f2(k, qq):
        f2send[k] = column_sum(qq).astype(BF16)
        f2_copy(k).start()

    def stage_f2():
        def wait(n):
            @pl.loop(0, rest_n)
            def _(z):
                @pl.when(z != rest)
                def _():
                    fz_copy(0, z, n).wait_recv()

        with_count(hub, None, wait)
        each_f2(send_f2)

    is_owner = jnp.logical_or(
        rest == 2, jnp.logical_and(rest == 1, jnp.logical_or(core == 0, y == 0))
    )

    def advance(n):
        pairs = [(state[i, 0], state[i, 1]) for i in range(2)]
        for _ in range(n):
            done = []
            for power, approx in pairs:
                both = dot3(jnp.concatenate([power, approx], axis=0), power)
                done.append((both[:BLK], approx + both[BLK:]))
            pairs = done
        return pairs

    def stage_f3():
        @pl.when(is_owner)
        def _():
            packed = column_sum(q)
            for k in range(3):
                f2_copy(k).wait_recv()
                packed = packed + f2recv[k].astype(F32)
            packed = packed * (1.0 / total)
            half = packed[:BLK]
            flip = half.T
            first = jnp.where(col >= row, half, flip)
            second = jnp.where(col > row, flip, jnp.where(col < row, half, packed[BLK:BLK + 1]))
            for i, factor in enumerate((first, second)):
                trace = jnp.sum(jnp.sum(factor * eye, axis=1, keepdims=True), axis=0, keepdims=True)
                damped = factor + (0.1 * (trace / BLK + 1e-06)) * eye
                peak = jnp.max(jnp.sum(jnp.abs(damped), axis=1, keepdims=True), axis=0, keepdims=True)
                scale = 1.0 / peak
                power = eye - scale * damped
                state[i, 1] = scale * (eye + power)
                state[i, 0] = dot3(power, power)

    def stage_newton(n, last):
        @pl.when(is_owner)
        def _():
            for i, (power, approx) in enumerate(advance(n)):
                if last:
                    inv_own[i] = (approx + dot3(approx, power)).astype(BF16)
                else:
                    state[i, 0] = power
                    state[i, 1] = approx

    def owned(owner):
        return jnp.logical_and(core == owner[0], rest == owner[1])

    def needs(t):
        return range(t * CBLK // zslots, (t * CBLK + CBLK - 1) // zslots + 1)

    a_sends = []
    for t in range(QBLK):
        for z in needs(t):
            for cc in range(2):
                if (cc, z) != A_OWNER[t][:2]:
                    a_sends.append((t, z, cc))

    def a_copy(i):
        t, z, cc = a_sends[i]
        return rcopy(inv_own.at[A_OWNER[t][2]], inv_a.at[t], inv_ss.at[i], inv_rs.at[t], at(y, x, z, cc))

    def g_half(e):
        return lax.div(q + 4 * e, CBLK)

    def gz_copy(e, z):
        return rcopy(
            inv_own.at[G_OWNER[e][2]], inv_g.at[lax.rem(q + 4 * e, CBLK)], gz_ss.at[e * rest_n + z],
            g_rs.at[lax.rem(q + 4 * e, CBLK)], at(y, x, z, g_half(e)),
        )

    def each_gz(body):
        for e in range(2):
            @pl.when(owned(G_OWNER[e]) if e == 0 else jnp.logical_and(owned(G_OWNER[e]), q < NG - 4))
            def _():
                @pl.loop(0, rest_n)
                def _(z):
                    @pl.when(jnp.logical_or(z != rest, g_half(e) != core))
                    def _():
                        body(e, z)

    def stage_inv():
        for i, (t, z, cc) in enumerate(a_sends):
            @pl.when(owned(A_OWNER[t]))
            def _():
                a_copy(i).start()
        each_gz(lambda e, z: gz_copy(e, z).start())
        for t in range(QBLK):
            if A_OWNER[t][1] in needs(t):
                @pl.when(owned(A_OWNER[t]))
                def _():
                    inv_a[t] = inv_own[A_OWNER[t][2]]

    def g_home(j):
        return lax.rem(core * CBLK + j, 4)

    def g_owned(j):
        late = core * CBLK + j >= 4
        return jnp.logical_or(
            jnp.logical_and(late, owned(G_OWNER[1])),
            jnp.logical_and(jnp.logical_not(late), owned(G_OWNER[0])),
        )

    def gp_copy(j, k):
        yy, xx = chips[k]
        return rcopy(inv_g.at[j], inv_g.at[j], gp_ss.at[3 * j + k], g_rs.at[j], at(yy, xx, rest, core))

    def stage_relay():
        for j in range(CBLK):
            @pl.when(q == g_home(j))
            def _():
                @pl.when(g_owned(j))
                def _():
                    inv_g[j] = inv_own[1 - core]

                @pl.when(jnp.logical_not(g_owned(j)))
                def _():
                    gp_copy(j, 0).wait_recv()

                for k in range(3):
                    gp_copy(j, k).start()

    m1[0].start()
    f1.start()
    m1[1].start()
    stage_own(0)
    stage_own(1)
    stage_own(2)
    stage_own(3)
    m1[2].start()
    stage_a(0)
    stage_f1()
    stage_a(1)
    m1[3].start()
    stage_b(0)
    stage_a(2)
    stage_f2()
    stage_b(1)
    stage_a(3)
    stage_z(0)
    stage_f3()
    stage_newton(3, False)
    stage_newton(3, True)
    stage_b(2)
    stage_inv()
    stage_z(1)
    stage_b(3)
    stage_z(2)
    stage_relay()
    stage_z(3)

    for j in range(CBLK):
        @pl.when(q != g_home(j))
        def _():
            gp_copy(j, 0).wait_recv()
    for t in range(QBLK):
        @pl.when(jnp.logical_and(
            jnp.logical_and(rest >= needs(t)[0], rest <= needs(t)[-1]),
            jnp.logical_not(owned(A_OWNER[t])),
        ))
        def _():
            rcopy(inv_own.at[0], inv_a.at[t], inv_ss.at[0], inv_rs.at[t], other).wait_recv()

    @pl.loop(0, rest_n)
    def _(z):
        @pl.when(z != rest)
        def _():
            for k in range(CH):
                z_copy(k, 0, z).wait_recv()

    square = jnp.zeros((1, 1), F32)
    for k in range(zslots):
        tile = rest * zslots + k
        m = jnp.concatenate(
            [sum(zrecv[j, z, k].astype(F32) for z in range(rest_n)) for j in range(CH)], axis=0
        )
        left = dot_t(inv_a[jnp.minimum(lax.div(tile, CBLK), QBLK - 1)], m.astype(BF16))
        hi, lo = split(left)
        ginv = inv_g[lax.rem(tile, CBLK)]
        part = dot(hi, ginv) + dot(lo, ginv)
        nat[k] = part
        square = square + jnp.sum(
            jnp.sum(part * part, axis=0, keepdims=True), axis=1, keepdims=True
        )
    qsend[...] = jnp.broadcast_to(square, (1, 128))

    def q_copy(p):
        return rcopy(qsend, qrecv.at[me], q_ss.at[0], q_rs.at[0], linear(p))

    rest_of = qrecv.at[pl.ds(0, devices - 1)]
    q_all = rcopy(rest_of, rest_of, q_ss.at[0], q_rs.at[0], other)

    def others(n, mine, body):
        @pl.loop(0, n)
        def _(p):
            @pl.when(p != mine)
            def _():
                body(p)

    others(devices, me, lambda p: q_copy(p).start())
    qrecv[me] = qsend[...]

    def each_piece(body):
        for xx in range(2):
            for i in range(QBLK * CBLK):
                t, c = divmod(i, CBLK)
                top = (2 * t + xx) * BLK

                @pl.when(jnp.logical_and(x == xx, rest == i // zslots))
                def _():
                    first = top // rows
                    for k in range(first, (top + BLK + rows - 1) // rows):
                        lo, hi = max(top, k * rows), min(top + BLK, (k + 1) * rows)
                        late = 0 if lo == k * rows else 1
                        body(i % zslots, c, k, lo - k * rows, lo - top, hi - lo, late,
                             i % zslots * pieces + k - first)

    def fin_copy(j, c, late, k):
        return rcopy(
            fin_send.at[j], fin_recv.at[core * CBLK + c, late], fin_ss.at[j],
            fin_rs.at[2 * (core * CBLK + c) + late], linear(y * half_n + k),
        )

    def send_piece(slot_k, c, k, above, start, count, late, j):
        parts = [nat[slot_k, start:start + count, :]]
        if above:
            parts.insert(0, jnp.zeros((above, BLK), F32))
        tail = fin_send.shape[1] - above - count
        if tail:
            parts.append(jnp.zeros((tail, BLK), F32))
        fin_send[j] = (jnp.concatenate(parts, axis=0) if len(parts) > 1 else parts[0]).astype(BF16)

        @pl.when(y * half_n + k != me)
        def _():
            fin_copy(j, c, late, k).start()

        @pl.when(y * half_n + k == me)
        def _():
            fin_recv[core * CBLK + c, late] = fin_send[j]

    each_piece(send_piece)

    k_me = lax.rem(me, half_n)
    t_me = lax.div(k_me * rows, BLK)
    straddles = lax.div(k_me * rows + rows - 1, BLK) > t_me
    mine_here = lax.div(me, half_n) == y
    for late in range(2):
        for c in range(NG):
            from_me = jnp.logical_and(
                jnp.logical_and(mine_here, core == c // CBLK),
                jnp.logical_and(
                    lax.rem(t_me + late, 2) == x,
                    lax.div(CBLK * lax.div(t_me + late, 2) + c % CBLK, zslots) == rest,
                ),
            )
            incoming = jnp.logical_not(from_me)
            if late:
                incoming = jnp.logical_and(straddles, incoming)

                @pl.when(jnp.logical_not(straddles))
                def _():
                    fin_recv[c, 1] = jnp.zeros(fin_recv.shape[2:], BF16)

            @pl.when(incoming)
            def _():
                pltpu.make_async_remote_copy(
                    src_ref=fin_send.at[0], dst_ref=fin_recv.at[c, late], send_sem=fin_ss.at[0],
                    recv_sem=fin_rs.at[2 * c + late], device_id=other, device_id_type=MESH,
                ).wait_recv()

    q_all.wait_recv()
    quad = jnp.sum(qrecv[...], axis=0)[:1, :1] / (D * R)
    factor_out = lax.rsqrt(quad + 1e-06)
    for c in range(NG):
        natural = fin_recv[c, 0].astype(F32) + fin_recv[c, 1].astype(F32)
        out_ref[:, c * BLK:(c + 1) * BLK] = natural[:rows, :] * factor_out

    f1.wait_send()
    for cp in m1 + list(ma.values()) + list(mb.values()):
        cp.wait_send()
    for s in range(2):
        with_count(rest != s + 1, s, lambda n: fz_copy(s, rest, n).wait_send())
    each_f2(lambda k, qq: f2_copy(k).wait_send())
    for i, (t, z, cc) in enumerate(a_sends):
        @pl.when(owned(A_OWNER[t]))
        def _():
            a_copy(i).wait_send()
    each_gz(lambda e, z: gz_copy(e, z).wait_send())
    for j in range(CBLK):
        @pl.when(q == g_home(j))
        def _():
            for k in range(3):
                gp_copy(j, k).wait_send()

    for k in range(CH):
        others(rest_n, rest, lambda z: z_copy(k, z, 0).wait_send())
    q_all.wait_send()

    def wait_piece(slot_k, c, k, above, start, count, late, j):
        @pl.when(y * half_n + k != me)
        def _():
            fin_copy(j, c, late, k).wait_send()

    each_piece(wait_piece)


def per_device(acts, cotangents, groups, width):
    tokens = acts.shape[0]
    devices = groups * width
    rest_n = devices // 8
    rows = D // devices
    padded = (rows + 15) // 16 * 16
    blk = (BLK, BLK)
    zslots = (QBLK * CBLK + rest_n - 1) // rest_n
    pieces = max(
        ((t + 1) * BLK + rows - 1) // rows - t * BLK // rows for t in range(2 * QBLK)
    )
    sems = [5, 1, 1, 2, rest_n, 3, 3, CH, CH, 2 * CH, 2 * CH, 2 * CH, 2 * CH,
            CH * rest_n, CH * rest_n, 2 * CBLK * QBLK, QBLK,
            2 * rest_n, 3 * CBLK, CBLK, zslots * pieces, 2 * NG, 1, 1]
    vm = pltpu.VMEM
    return pl.pallas_call(
        functools.partial(kernel, groups, width, tokens * devices, rows),
        out_shape=jax.ShapeDtypeStruct((rows, R), F32),
        in_specs=[pl.BlockSpec(memory_space=pl.ANY)] * 2,
        out_specs=pl.BlockSpec(memory_space=pltpu.VMEM),
        scratch_shapes=[
            vm((tokens, D), BF16),
            vm((tokens, R), BF16),
            vm((NA, BLK, tokens), BF16),
            vm((2, 4, 2, PROWS, BLK), BF16),
            vm((4, 2, PROWS, BLK), BF16),
            vm((2, 4, PROWS, BLK), BF16),
            vm((rest_n, 4, PROWS, BLK), BF16),
            vm((3, PROWS, BLK), BF16),
            vm((3, PROWS, BLK), BF16),
            vm((CH, 2, 2, 2, SROWS, CCOLS), BF16),
            vm((CH, 2, 2, 2, SROWS, CCOLS), BF16),
            vm((CH, 2, 2, 2, SROWS, CCOLS), F32),
            vm((CH, 2, 2, SROWS, CCOLS), BF16),
            vm((CH, 2, 2, SROWS, CCOLS), BF16),
            vm((CH, 2, SROWS, CCOLS), BF16),
            vm((CH, 2, SROWS, CCOLS), BF16),
            vm((CH, rest_n, zslots, PART, BLK), BF16),
            vm((CH, rest_n, zslots, PART, BLK), BF16),
            vm((2, 2) + blk, F32),
            vm((2,) + blk, BF16),
            vm((QBLK,) + blk, BF16),
            vm((CBLK,) + blk, BF16),
            vm((zslots,) + blk, F32),
            vm((zslots * pieces, padded, BLK), BF16),
            vm((NG, 2, padded, BLK), BF16),
            vm((1, 128), F32),
            vm((devices, 1, 128), F32),
            pltpu.SemaphoreType.REGULAR((8,)),
        ] + [pltpu.SemaphoreType.DMA((n,)) for n in sems],
        compiler_params=pltpu.CompilerParams(
            collective_id=0, has_side_effects=True, vmem_limit_bytes=63 * 1024 * 1024
        ),
    )(acts, cotangents)


def solution(mesh):
    groups, width = mesh.shape["grp"], mesh.shape["dp"]
    spec = P(("grp", "dp"), None)
    return jax.shard_map(
        functools.partial(per_device, groups=groups, width=width),
        mesh=mesh, in_specs=(spec, spec), out_specs=spec, check_vma=False,
    )
```

```python
import functools

import jax
import jax.numpy as jnp
from jax import lax
from jax.experimental import pallas as pl
from jax.experimental.pallas import tpu as pltpu
from jax.sharding import PartitionSpec as P

D = 2560
R = 768
BLK = 128
ITERS = 8
NA = D // BLK
NG = R // BLK
QROWS = D // 4
QBLK = QROWS // BLK
CH = 4
PART = BLK // CH
SUB = PART // 2
SROWS = QBLK * SUB
CCOLS = R // 2
CBLK = CCOLS // BLK
PROWS = BLK + 16
A_OWNER = ((0, 1, 0), (0, 1, 1), (1, 2, 0), (1, 2, 1), (0, 2, 0))
G_OWNER = ((0, 2, 1), (1, 1, 0))
MESH = pl.DeviceIdType.MESH
F32 = jnp.float32
BF16 = jnp.bfloat16


def dot(a, b):
    return jnp.dot(a, b, preferred_element_type=F32)


def dot_t(a, b):
    return lax.dot_general(a, b, (((0,), (0,)), ((), ())), preferred_element_type=F32)


def split(a):
    hi = a.astype(BF16)
    return hi, (a - hi.astype(F32)).astype(BF16)


def dot3(a, b):
    ah, al = split(a)
    bh, bl = split(b)
    both = dot(
        jnp.concatenate([ah, al], axis=1),
        jnp.concatenate(
            [jnp.concatenate([bh, bl], axis=1), jnp.concatenate([bh, jnp.zeros_like(bh)], axis=1)],
            axis=0,
        ),
    )
    return both[:, :BLK] + both[:, BLK:]


def kernel(
    groups, width, total, rows,
    x_hbm, g_hbm, out_ref,
    x_ref, g_ref, xt, fpart, f1recv, fzsend, fzrecv, f2send, f2recv,
    m1send, m1recv, mown, masend, m2a, mbsend, m2b,
    zsend, zrecv, state, inv_own, inv_a, inv_g, nat, fin_send, fin_recv, qsend, qrecv,
    know, in_sem,
    f1_ss, f1_rs, fz_ss, fz_rs, f2_ss, f2_rs, m1_ss, m1_rs, ma_ss, ma_rs,
    mb_ss, mb_rs, z_ss, z_rs, inv_ss, inv_rs, gz_ss, gp_ss, g_rs, fin_ss, fin_rs, q_ss, q_rs,
):
    devices = groups * width
    rest_n = devices // 8
    half_n = devices // 2
    zslots = zsend.shape[1]
    pieces = fin_send.shape[0] // zslots
    dp_rest = width // 4
    gi = lax.axis_index("grp")
    di = lax.axis_index("dp")
    me = gi * width + di
    core = lax.rem(di, 2)
    x = lax.rem(lax.div(di, 2), 2)
    y = lax.rem(gi, 2)
    q = 2 * y + x
    rest = lax.div(gi, 2) * dp_rest + lax.div(di, 4)

    def at(yy, xx, zz, cc):
        return (
            lax.div(zz, dp_rest) * 2 + yy,
            lax.rem(zz, dp_rest) * 4 + xx * 2 + cc,
        )

    def linear(d):
        return (lax.div(d, width), lax.rem(d, width))

    def rcopy(src, dst, ss, rs, dev):
        return pltpu.make_async_remote_copy(
            src_ref=src, dst_ref=dst, send_sem=ss, recv_sem=rs,
            device_id=dev, device_id_type=MESH,
        )

    g_in = pltpu.make_async_copy(g_hbm, g_ref, in_sem.at[4])
    g_in.start()
    x_in = []
    for i in range(4):
        cols = pl.ds(i * QROWS, QROWS)
        x_in.append(pltpu.make_async_copy(x_hbm.at[:, cols], x_ref.at[:, cols], in_sem.at[i]))
        x_in[i].start()

    barrier = pltpu.get_barrier_semaphore()

    def greet(dev):
        pl.semaphore_signal(barrier, inc=1, device_id=dev, device_id_type=MESH)

    greet(at(y, x, rest, 1 - core))
    greet(at(y, 1 - x, rest, core))
    greet(at(1 - y, x, rest, core))

    def near_z(reach, body):
        @pl.when(rest >= reach)
        def _():
            body(rest - reach)

        @pl.when(rest + reach < rest_n)
        def _():
            body(rest + reach)

    def sides(reach):
        return (rest >= reach).astype(jnp.int32) + (rest + reach < rest_n).astype(jnp.int32)

    near_z(1, lambda z: greet(at(y, x, z, core)))
    rounds = (rest_n - 2).bit_length()
    hub_rounds = (max(rest_n - 3, 1)).bit_length()

    def tell(r):
        near_z(1 << r, lambda z: pl.semaphore_signal(
            know.at[r], inc=1, device_id=at(y, x, z, core), device_id_type=MESH
        ))

    def hear(first, last):
        for r in range(first, last):
            pl.semaphore_wait(know.at[r], sides(1 << r))
            if r + 1 < rounds:
                tell(r + 1)

    zero = jnp.zeros((BLK, BLK), BF16)
    g_in.wait()
    g_other = g_ref[:, pl.ds(pl.multiple_of((1 - core) * CCOLS, BLK), CCOLS)]
    g_mine = g_ref[:, pl.ds(pl.multiple_of(core * CCOLS, BLK), CCOLS)]
    for i in range(QBLK * CBLK, zslots * rest_n):
        for k in range(CH):
            zsend[k, i // zslots, i % zslots] = zero[:PART]

    def scatter(ref, yq, xq, t, value):
        for k in range(CH):
            for h in range(2):
                major, minor = (xq, yq) if h == 0 else (yq, xq)
                start = k * PART + h * SUB
                ref[k, h, major, minor, t * SUB:(t + 1) * SUB, :] = value[start:start + SUB]

    if zslots * rest_n > QBLK * CBLK:
        @pl.when(rest * zslots >= QBLK * CBLK)
        def _():
            inv_a[QBLK - 1] = zero

    row = lax.broadcasted_iota(jnp.int32, (BLK, BLK), 0)
    col = lax.broadcasted_iota(jnp.int32, (BLK, BLK), 1)
    eye = (row == col).astype(F32)

    def pack(ref, first, second):
        ref[:BLK, :] = jnp.where(col >= row, first, second).astype(BF16)
        diag = jnp.sum(second * eye, axis=0, keepdims=True)
        ref[BLK:, :] = jnp.broadcast_to(diag, (PROWS - BLK, BLK)).astype(BF16)

    def gram(c):
        gb = g_ref[:, c * BLK:(c + 1) * BLK]
        return dot_t(gb, gb)

    for qq in range(NG - 4):
        last = gram(4 + qq)
        pack(fpart.at[1, qq, 0], last, last)
    for qq in range(NG - 4, 4):
        fpart[1, qq, 0] = jnp.zeros((PROWS, BLK), BF16)

    held = {}
    for part in range(4):
        x_in[part].wait()
        for b in range(part * QBLK, (part + 1) * QBLK):
            yq, xq, t = b // (2 * QBLK), b % 2, b % (2 * QBLK) // 2
            qq = 2 * yq + xq
            xb = x_ref[:, b * BLK:(b + 1) * BLK]
            xbt = xb.T
            xt[b] = xbt
            held[t] = held.get(t, {})
            held[t][qq] = dot(xbt, xb)
            if t == 1:
                pack(fpart.at[0, qq, 0], held[0][qq], held[1][qq])
            elif t == 3:
                pack(fpart.at[1, qq, 1], held[2][qq], held[3][qq])
            elif t == 4:
                pack(fpart.at[0, qq, 1], held[4][qq], gram(qq))
    for b in range(NA):
        yq, xq, t = b // (2 * QBLK), b % 2, b % (2 * QBLK) // 2
        scatter(m1send, yq, xq, t, dot(xt[b], g_other).astype(BF16))

    pl.semaphore_wait(barrier, 3 + sides(1))
    tell(0)
    other = at(y, x, rest, 1 - core)
    at_x = at(y, 1 - x, rest, core)
    at_y = at(1 - y, x, rest, core)
    f1 = rcopy(fpart.at[1 - core], f1recv, f1_ss.at[0], f1_rs.at[0], other)
    m1 = [rcopy(m1send.at[k], m1recv.at[k], m1_ss.at[k], m1_rs.at[k], other) for k in range(CH)]

    def stage_own(part):
        for b in range(part * QBLK, (part + 1) * QBLK):
            yq, xq, t = b // (2 * QBLK), b % 2, b % (2 * QBLK) // 2
            scatter(mown, yq, xq, t, dot(xt[b], g_mine))

    def summed(k, h, major, minor):
        return mown[k, h, major, minor] + m1recv[k, h, major, minor].astype(F32)

    side = (x, y)
    near = (at_x, at_y)
    ma, mb = {}, {}

    def stage_a(k):
        m1[k].wait_recv()
        for h in range(2):
            for minor in range(2):
                masend[k, h, minor] = summed(k, h, 1 - side[h], minor).astype(BF16)
            ma[k, h] = rcopy(
                masend.at[k, h], m2a.at[k, h], ma_ss.at[2 * k + h], ma_rs.at[2 * k + h], near[h]
            )
            ma[k, h].start()

    def stage_b(k):
        for h in range(2):
            ma[k, h].wait_recv()
            minor = 1 - side[1 - h]
            mbsend[k, h] = (
                summed(k, h, side[h], minor) + m2a[k, h, minor].astype(F32)
            ).astype(BF16)
            mb[k, h] = rcopy(
                mbsend.at[k, h], m2b.at[k, h], mb_ss.at[2 * k + h], mb_rs.at[2 * k + h], near[1 - h]
            )
            mb[k, h].start()

    def z_copy(k, dst, src):
        return rcopy(
            zsend.at[k, dst], zrecv.at[k, src],
            z_ss.at[k * rest_n + dst], z_rs.at[k * rest_n + src], at(y, x, dst, core),
        )

    chips = [(y, 1 - x), (1 - y, x), (1 - y, 1 - x)]

    def stage_z(k):
        if k == 0:
            hear(hub_rounds, rounds)
        for h in range(2):
            mb[k, h].wait_recv()
            minor = side[1 - h]
            value = (
                summed(k, h, side[h], minor) + m2a[k, h, minor].astype(F32) + m2b[k, h].astype(F32)
            ) * (1.0 / total)
            value = value.astype(BF16)
            for i in range(QBLK * CBLK):
                t, c = divmod(i, CBLK)
                zsend[k, i // zslots, i % zslots, h * SUB:(h + 1) * SUB, :] = (
                    value[t * SUB:(t + 1) * SUB, c * BLK:(c + 1) * BLK]
                )

        @pl.loop(0, rest_n)
        def _(z):
            @pl.when(z != rest)
            def _():
                z_copy(k, z, rest).start()

        zrecv[k, rest] = zsend[k, rest]

    def f1_sum(qq, s):
        return fpart[core, qq, s].astype(F32) + f1recv[qq, s].astype(F32)


    def f2_copy(k, s):
        yy, xx = chips[k]
        i = 2 * k + s
        return rcopy(f2send.at[k, s], f2recv.at[k, s], f2_ss.at[i], f2_rs.at[i], at(yy, xx, rest, core))

    def fz_copy(s, src, n):
        return rcopy(
            fzsend.at[s, pl.ds(0, n)], fzrecv.at[src, pl.ds(0, n)], fz_ss.at[s], fz_rs.at[src],
            at(y, x, s + 1, core),
        )

    def with_count(here, s, body):
        late = core if s is None else core * (1 - s)
        if s is None:
            late = core * (2 - rest)

        @pl.when(jnp.logical_and(here, late == 1))
        def _():
            body(NG - 4)

        @pl.when(jnp.logical_and(here, late != 1))
        def _():
            body(4)

    def stage_f1():
        hear(0, hub_rounds)
        f1.wait_recv()
        for s in range(2):
            for qq in range(4):
                fzsend[s, qq] = f1_sum(qq, s).astype(BF16)
            with_count(rest != s + 1, s, lambda n: fz_copy(s, rest, n).start())

            @pl.when(rest == s + 1)
            def _():
                fzrecv[s + 1] = fzsend[s]

    hub = jnp.logical_or(rest == 1, rest == 2)

    def column_sum(qq):
        f = fzrecv[0, qq].astype(F32)
        for z in range(1, rest_n):
            f = f + fzrecv[z, qq].astype(F32)
        return f

    def f2_copy(k):
        yy, xx = chips[k]
        return rcopy(f2send.at[k], f2recv.at[k], f2_ss.at[k], f2_rs.at[k], at(yy, xx, rest, core))

    def each_f2(body):
        for k, (yy, xx) in enumerate(chips):
            @pl.when(jnp.logical_or(
                rest == 2, jnp.logical_and(rest == 1, jnp.logical_or(core == 0, yy == 0))
            ))
            def _():
                body(k, 2 * yy + xx)

    def send_f2(k, qq):
        f2send[k] = column_sum(qq).astype(BF16)
        f2_copy(k).start()

    def stage_f2():
        def wait(n):
            @pl.loop(0, rest_n)
            def _(z):
                @pl.when(z != rest)
                def _():
                    fz_copy(0, z, n).wait_recv()

        with_count(hub, None, wait)
        each_f2(send_f2)

    is_owner = jnp.logical_or(
        rest == 2, jnp.logical_and(rest == 1, jnp.logical_or(core == 0, y == 0))
    )

    def advance(n):
        pairs = [(state[i, 0], state[i, 1]) for i in range(2)]
        for _ in range(n):
            done = []
            for power, approx in pairs:
                both = dot3(jnp.concatenate([power, approx], axis=0), power)
                done.append((both[:BLK], approx + both[BLK:]))
            pairs = done
        return pairs

    def stage_f3():
        @pl.when(is_owner)
        def _():
            packed = column_sum(q)
            for k in range(3):
                f2_copy(k).wait_recv()
                packed = packed + f2recv[k].astype(F32)
            packed = packed * (1.0 / total)
            half = packed[:BLK]
            flip = half.T
            first = jnp.where(col >= row, half, flip)
            second = jnp.where(col > row, flip, jnp.where(col < row, half, packed[BLK:BLK + 1]))
            for i, factor in enumerate((first, second)):
                trace = jnp.sum(jnp.sum(factor * eye, axis=1, keepdims=True), axis=0, keepdims=True)
                damped = factor + (0.1 * (trace / BLK + 1e-06)) * eye
                peak = jnp.max(jnp.sum(jnp.abs(damped), axis=1, keepdims=True), axis=0, keepdims=True)
                scale = 1.0 / peak
                power = eye - scale * damped
                state[i, 1] = scale * (eye + power)
                state[i, 0] = dot3(power, power)

    def stage_newton(n, last):
        @pl.when(is_owner)
        def _():
            for i, (power, approx) in enumerate(advance(n)):
                if last:
                    inv_own[i] = (approx + dot3(approx, power)).astype(BF16)
                else:
                    state[i, 0] = power
                    state[i, 1] = approx

    def owned(owner):
        return jnp.logical_and(core == owner[0], rest == owner[1])

    def needs(t):
        return range(t * CBLK // zslots, (t * CBLK + CBLK - 1) // zslots + 1)

    a_sends = []
    for t in range(QBLK):
        for z in needs(t):
            for cc in range(2):
                if (cc, z) != A_OWNER[t][:2]:
                    a_sends.append((t, z, cc))

    def a_copy(i):
        t, z, cc = a_sends[i]
        return rcopy(inv_own.at[A_OWNER[t][2]], inv_a.at[t], inv_ss.at[i], inv_rs.at[t], at(y, x, z, cc))

    def g_half(e):
        return lax.div(q + 4 * e, CBLK)

    def gz_copy(e, z):
        return rcopy(
            inv_own.at[G_OWNER[e][2]], inv_g.at[lax.rem(q + 4 * e, CBLK)], gz_ss.at[e * rest_n + z],
            g_rs.at[lax.rem(q + 4 * e, CBLK)], at(y, x, z, g_half(e)),
        )

    def each_gz(body):
        for e in range(2):
            @pl.when(owned(G_OWNER[e]) if e == 0 else jnp.logical_and(owned(G_OWNER[e]), q < NG - 4))
            def _():
                @pl.loop(0, rest_n)
                def _(z):
                    @pl.when(jnp.logical_or(z != rest, g_half(e) != core))
                    def _():
                        body(e, z)

    def stage_inv():
        for i, (t, z, cc) in enumerate(a_sends):
            @pl.when(owned(A_OWNER[t]))
            def _():
                a_copy(i).start()
        each_gz(lambda e, z: gz_copy(e, z).start())
        for t in range(QBLK):
            if A_OWNER[t][1] in needs(t):
                @pl.when(owned(A_OWNER[t]))
                def _():
                    inv_a[t] = inv_own[A_OWNER[t][2]]

    def g_home(j):
        return lax.rem(core * CBLK + j, 4)

    def g_owned(j):
        late = core * CBLK + j >= 4
        return jnp.logical_or(
            jnp.logical_and(late, owned(G_OWNER[1])),
            jnp.logical_and(jnp.logical_not(late), owned(G_OWNER[0])),
        )

    def gp_copy(j, k):
        yy, xx = chips[k]
        return rcopy(inv_g.at[j], inv_g.at[j], gp_ss.at[3 * j + k], g_rs.at[j], at(yy, xx, rest, core))

    def stage_relay():
        for j in range(CBLK):
            @pl.when(q == g_home(j))
            def _():
                @pl.when(g_owned(j))
                def _():
                    inv_g[j] = inv_own[1 - core]

                @pl.when(jnp.logical_not(g_owned(j)))
                def _():
                    gp_copy(j, 0).wait_recv()

                for k in range(3):
                    gp_copy(j, k).start()

    m1[0].start()
    f1.start()
    m1[1].start()
    stage_own(0)
    stage_own(1)
    stage_own(2)
    stage_own(3)
    m1[2].start()
    stage_a(0)
    stage_f1()
    stage_a(1)
    m1[3].start()
    stage_b(0)
    stage_a(2)
    stage_f2()
    stage_b(1)
    stage_a(3)
    stage_z(0)
    stage_f3()
    stage_newton(3, False)
    stage_newton(3, True)
    stage_b(2)
    stage_inv()
    stage_z(1)
    stage_b(3)
    stage_z(2)
    stage_relay()
    stage_z(3)

    for j in range(CBLK):
        @pl.when(q != g_home(j))
        def _():
            gp_copy(j, 0).wait_recv()
    for t in range(QBLK):
        @pl.when(jnp.logical_and(
            jnp.logical_and(rest >= needs(t)[0], rest <= needs(t)[-1]),
            jnp.logical_not(owned(A_OWNER[t])),
        ))
        def _():
            rcopy(inv_own.at[0], inv_a.at[t], inv_ss.at[0], inv_rs.at[t], other).wait_recv()

    @pl.loop(0, rest_n)
    def _(z):
        @pl.when(z != rest)
        def _():
            for k in range(CH):
                z_copy(k, 0, z).wait_recv()

    square = jnp.zeros((BLK, BLK), F32)
    for k in range(zslots):
        tile = rest * zslots + k
        m = jnp.concatenate(
            [sum(zrecv[j, z, k].astype(F32) for z in range(rest_n)) for j in range(CH)], axis=0
        )
        left = dot_t(inv_a[jnp.minimum(lax.div(tile, CBLK), QBLK - 1)], m.astype(BF16))
        hi, lo = split(left)
        ginv = inv_g[lax.rem(tile, CBLK)]
        part = dot(hi, ginv) + dot(lo, ginv)
        nat[k] = part
        square = square + part * part
    qsend[...] = jnp.sum(square, axis=0, keepdims=True)

    def q_copy(p):
        return rcopy(qsend, qrecv.at[me], q_ss.at[0], q_rs.at[0], linear(p))

    rest_of = qrecv.at[pl.ds(0, devices - 1)]
    q_all = rcopy(rest_of, rest_of, q_ss.at[0], q_rs.at[0], other)

    def others(n, mine, body):
        @pl.loop(0, n)
        def _(p):
            @pl.when(p != mine)
            def _():
                body(p)

    others(devices, me, lambda p: q_copy(p).start())
    qrecv[me] = qsend[...]

    def each_piece(body):
        for xx in range(2):
            for i in range(QBLK * CBLK):
                t, c = divmod(i, CBLK)
                top = (2 * t + xx) * BLK

                @pl.when(jnp.logical_and(x == xx, rest == i // zslots))
                def _():
                    first = top // rows
                    for k in range(first, (top + BLK + rows - 1) // rows):
                        lo, hi = max(top, k * rows), min(top + BLK, (k + 1) * rows)
                        late = 0 if lo == k * rows else 1
                        body(i % zslots, c, k, lo - k * rows, lo - top, hi - lo, late,
                             i % zslots * pieces + k - first)

    def fin_copy(j, c, late, k):
        return rcopy(
            fin_send.at[j], fin_recv.at[core * CBLK + c, late], fin_ss.at[j],
            fin_rs.at[2 * (core * CBLK + c) + late], linear(y * half_n + k),
        )

    def send_piece(slot_k, c, k, above, start, count, late, j):
        parts = [nat[slot_k, start:start + count, :]]
        if above:
            parts.insert(0, jnp.zeros((above, BLK), F32))
        tail = fin_send.shape[1] - above - count
        if tail:
            parts.append(jnp.zeros((tail, BLK), F32))
        fin_send[j] = (jnp.concatenate(parts, axis=0) if len(parts) > 1 else parts[0]).astype(BF16)

        @pl.when(y * half_n + k != me)
        def _():
            fin_copy(j, c, late, k).start()

        @pl.when(y * half_n + k == me)
        def _():
            fin_recv[core * CBLK + c, late] = fin_send[j]

    each_piece(send_piece)

    k_me = lax.rem(me, half_n)
    t_me = lax.div(k_me * rows, BLK)
    straddles = lax.div(k_me * rows + rows - 1, BLK) > t_me
    mine_here = lax.div(me, half_n) == y
    for late in range(2):
        for c in range(NG):
            from_me = jnp.logical_and(
                jnp.logical_and(mine_here, core == c // CBLK),
                jnp.logical_and(
                    lax.rem(t_me + late, 2) == x,
                    lax.div(CBLK * lax.div(t_me + late, 2) + c % CBLK, zslots) == rest,
                ),
            )
            incoming = jnp.logical_not(from_me)
            if late:
                incoming = jnp.logical_and(straddles, incoming)

                @pl.when(jnp.logical_not(straddles))
                def _():
                    fin_recv[c, 1] = jnp.zeros(fin_recv.shape[2:], BF16)

            @pl.when(incoming)
            def _():
                pltpu.make_async_remote_copy(
                    src_ref=fin_send.at[0], dst_ref=fin_recv.at[c, late], send_sem=fin_ss.at[0],
                    recv_sem=fin_rs.at[2 * c + late], device_id=other, device_id_type=MESH,
                ).wait_recv()

    q_all.wait_recv()
    quad = jnp.sum(jnp.sum(qrecv[...], axis=0), axis=1, keepdims=True) / (D * R)
    factor_out = lax.rsqrt(quad + 1e-06)
    for c in range(NG):
        natural = fin_recv[c, 0].astype(F32) + fin_recv[c, 1].astype(F32)
        out_ref[:, c * BLK:(c + 1) * BLK] = natural[:rows, :] * factor_out

    f1.wait_send()
    for cp in m1 + list(ma.values()) + list(mb.values()):
        cp.wait_send()
    for s in range(2):
        with_count(rest != s + 1, s, lambda n: fz_copy(s, rest, n).wait_send())
    each_f2(lambda k, qq: f2_copy(k).wait_send())
    for i, (t, z, cc) in enumerate(a_sends):
        @pl.when(owned(A_OWNER[t]))
        def _():
            a_copy(i).wait_send()
    each_gz(lambda e, z: gz_copy(e, z).wait_send())
    for j in range(CBLK):
        @pl.when(q == g_home(j))
        def _():
            for k in range(3):
                gp_copy(j, k).wait_send()

    for k in range(CH):
        others(rest_n, rest, lambda z: z_copy(k, z, 0).wait_send())
    q_all.wait_send()

    def wait_piece(slot_k, c, k, above, start, count, late, j):
        @pl.when(y * half_n + k != me)
        def _():
            fin_copy(j, c, late, k).wait_send()

    each_piece(wait_piece)


def per_device(acts, cotangents, groups, width):
    tokens = acts.shape[0]
    devices = groups * width
    rest_n = devices // 8
    rows = D // devices
    padded = (rows + 15) // 16 * 16
    blk = (BLK, BLK)
    zslots = (QBLK * CBLK + rest_n - 1) // rest_n
    pieces = max(
        ((t + 1) * BLK + rows - 1) // rows - t * BLK // rows for t in range(2 * QBLK)
    )
    sems = [5, 1, 1, 2, rest_n, 3, 3, CH, CH, 2 * CH, 2 * CH, 2 * CH, 2 * CH,
            CH * rest_n, CH * rest_n, 2 * CBLK * QBLK, QBLK,
            2 * rest_n, 3 * CBLK, CBLK, zslots * pieces, 2 * NG, 1, 1]
    vm = pltpu.VMEM
    return pl.pallas_call(
        functools.partial(kernel, groups, width, tokens * devices, rows),
        out_shape=jax.ShapeDtypeStruct((rows, R), F32),
        in_specs=[pl.BlockSpec(memory_space=pl.ANY)] * 2,
        out_specs=pl.BlockSpec(memory_space=pltpu.VMEM),
        scratch_shapes=[
            vm((tokens, D), BF16),
            vm((tokens, R), BF16),
            vm((NA, BLK, tokens), BF16),
            vm((2, 4, 2, PROWS, BLK), BF16),
            vm((4, 2, PROWS, BLK), BF16),
            vm((2, 4, PROWS, BLK), BF16),
            vm((rest_n, 4, PROWS, BLK), BF16),
            vm((3, PROWS, BLK), BF16),
            vm((3, PROWS, BLK), BF16),
            vm((CH, 2, 2, 2, SROWS, CCOLS), BF16),
            vm((CH, 2, 2, 2, SROWS, CCOLS), BF16),
            vm((CH, 2, 2, 2, SROWS, CCOLS), F32),
            vm((CH, 2, 2, SROWS, CCOLS), BF16),
            vm((CH, 2, 2, SROWS, CCOLS), BF16),
            vm((CH, 2, SROWS, CCOLS), BF16),
            vm((CH, 2, SROWS, CCOLS), BF16),
            vm((CH, rest_n, zslots, PART, BLK), BF16),
            vm((CH, rest_n, zslots, PART, BLK), BF16),
            vm((2, 2) + blk, F32),
            vm((2,) + blk, BF16),
            vm((QBLK,) + blk, BF16),
            vm((CBLK,) + blk, BF16),
            vm((zslots,) + blk, F32),
            vm((zslots * pieces, padded, BLK), BF16),
            vm((NG, 2, padded, BLK), BF16),
            vm((1, 128), F32),
            vm((devices, 1, 128), F32),
            pltpu.SemaphoreType.REGULAR((8,)),
        ] + [pltpu.SemaphoreType.DMA((n,)) for n in sems],
        compiler_params=pltpu.CompilerParams(
            collective_id=0, has_side_effects=True, vmem_limit_bytes=63 * 1024 * 1024
        ),
    )(acts, cotangents)


def solution(mesh):
    groups, width = mesh.shape["grp"], mesh.shape["dp"]
    spec = P(("grp", "dp"), None)
    return jax.shard_map(
        functools.partial(per_device, groups=groups, width=width),
        mesh=mesh, in_specs=(spec, spec), out_specs=spec, check_vma=False,
    )
```
